32 devices in a mesh: row: 8 (over y, x, core), col: 4 (over z).
Axes of the slice: x: 2, y: 2, z: 4, core: 2. Of those that a mesh axis runs over, the one named last changes fastest.
Arguments:
- activations: bfloat16 [256, 16384], P('col', 'row'), may hold values from -6 to 6
- grad_out: bfloat16 [256, 16384], P('col', 'row'), may hold values from -1.5 to 1.5
- first_blocks: bfloat16 [8, 4, 384, 128, 128], P('row', 'col'), may hold values from -0.125 to 0.125
- first_coords: int32 [8, 4, 384, 2], P('row', 'col'), may hold values from -1 to 511, as said below
- second_blocks: bfloat16 [4, 8, 384, 128, 128], P('col', 'row'), may hold values from -0.0625 to 0.0625
- second_coords: int32 [4, 8, 384, 2], P('col', 'row'), may hold values from -1 to 511, as said below
Outputs:
- output: float32 [256, 16384], P('col', 'row')
- grad_input: float32 [256, 16384], P('col', 'row')
- grad_first: bfloat16 [8, 4, 384, 128, 128], P('row', 'col')
- grad_second: bfloat16 [4, 8, 384, 128, 128], P('col', 'row')
The draws below stay inside these ranges and needn't reach their ends.
Inputs may be any that keep to these rules, and one draw needn't show every extreme that they name: `first_coords`: tile [a, b] lists, once each, exactly the nonzero blocks of W1 whose block row lies in a * 16 to a * 16 + 15 and whose block column lies in b * 128 to b * 128 + 127, in increasing order of block row and then block column; the remaining of its 384 slots hold -1 in both coordinates. Some tile fills all 384 slots. `second_coords`: tile [a, b] lists, once each, exactly the nonzero blocks of W2 whose block row lies in a * 128 to a * 128 + 127 and whose block column lies in b * 16 to b * 16 + 15, in increasing order of block row and then block column; the remaining of its 384 slots hold -1 in both coordinates. Some tile fills all 384 slots.
All inputs are finite; a program needn't handle non-finite values.
Results may differ from the reference program's by a relative error of at most 0.005.
Values may be sent and summed in bfloat16 or wider, within the bound.
A program may use at most 320 MiB of HBM per device.

```python
import jax
import jax.numpy as jnp
from jax import lax

D = 16384
FF = 65536
BLK = 128
TOKENS = 256
DB = 128
FB = 512
RB = 16
CB = 128
CAP = 384
N_ROW = 8
N_COL = 4


def single_bit(values):
    return jnp.bitwise_and(values, values - 1) == 0


def butterfly_pattern(key, rows_total, cols_total, rows_tile, cols_tile, rows_model):
    model_xor = jax.random.randint(jax.random.fold_in(key, 1), (), 0, DB, dtype=jnp.int32)
    hidden_xor = jax.random.randint(jax.random.fold_in(key, 2), (), 0, FB, dtype=jnp.int32)
    group_count = FB // CB
    group_table = jax.random.randint(jax.random.fold_in(key, 3), (group_count,), 0, DB, dtype=jnp.int32)
    row_groups = rows_total // rows_tile
    col_groups = cols_total // cols_tile
    full_shape = (row_groups, col_groups, rows_tile, cols_tile)
    grid_rows = jnp.broadcast_to(jnp.arange(row_groups, dtype=jnp.int32)[:, None, None, None] * rows_tile + jnp.arange(rows_tile, dtype=jnp.int32)[None, None, :, None], full_shape)
    grid_cols = jnp.broadcast_to(jnp.arange(col_groups, dtype=jnp.int32)[None, :, None, None] * cols_tile + jnp.arange(cols_tile, dtype=jnp.int32)[None, None, None, :], full_shape)
    if rows_model:
        model_index, hidden_index = (grid_rows, grid_cols)
    else:
        model_index, hidden_index = (grid_cols, grid_rows)
    group_xor = jnp.take(group_table, hidden_index // CB)
    offset = jnp.right_shift(jnp.bitwise_xor(hidden_index, hidden_xor), 2)
    differ = jnp.bitwise_xor(offset, jnp.bitwise_xor(model_index, jnp.bitwise_xor(model_xor, group_xor)))
    nonzero = single_bit(differ) | single_bit(jnp.bitwise_xor(differ, DB - 1))
    tile_span = rows_tile * cols_tile
    nonzero_flags = nonzero.reshape(row_groups, col_groups, tile_span).astype(jnp.int32)
    scores = (1 - nonzero_flags) * tile_span + jnp.arange(tile_span, dtype=jnp.int32)
    ranking = jnp.argsort(scores, axis=-1)[..., :CAP]
    is_kept = jnp.take_along_axis(nonzero_flags, ranking, axis=-1) > 0
    rows_flat = jnp.take_along_axis(grid_rows.reshape(row_groups, col_groups, tile_span), ranking, axis=-1)
    cols_flat = jnp.take_along_axis(grid_cols.reshape(row_groups, col_groups, tile_span), ranking, axis=-1)
    coords = jnp.stack([jnp.where(is_kept, rows_flat, -1), jnp.where(is_kept, cols_flat, -1)], axis=-1)
    return coords.astype(jnp.int32)


def draw_first_coords(key, part):
    return butterfly_pattern(jax.random.fold_in(key, 101), DB, FB, RB, CB, True)


def draw_second_coords(key, part):
    return butterfly_pattern(jax.random.fold_in(key, 202), FB, DB, CB, RB, False)


def shard_levels(key, shape, split, low, top_value):
    factor_of = 1.0
    for position, blocks in split:
        draws = jax.random.uniform(jax.random.fold_in(jax.random.fold_in(key, 6), position), (blocks,), jnp.float32, low / len(split), top_value / len(split))
        factor_of = factor_of * jnp.repeat(jnp.exp(draws), shape[position] // blocks).reshape((-1,) + (1,) * (len(shape) - 1 - position))
    return factor_of


def gaussian(key, extent, deviation, reach, shards=(), kind=jnp.bfloat16):
    values = jax.random.normal(key, extent, jnp.float32) * deviation
    if len(shards) > 0:
        values = shard_levels(key, extent, shards, -0.22, 0.18) * values
    return jnp.clip(values, min=-reach, max=reach).astype(kind)


def setup_inputs(seed: int = 0) -> dict:
    arg_keys = jax.random.split(jax.random.key(seed), 7)
    activations = gaussian(arg_keys[0], (TOKENS, D), 1.0, 6.0, ((0, 4), (1, 8)))
    grad_out = gaussian(arg_keys[1], (TOKENS, D), 0.25, 1.5, ((0, 4), (1, 8)))
    first_blocks = gaussian(arg_keys[2], (N_ROW, N_COL, CAP, BLK, BLK), (D // 8) ** -0.5, 0.125, ((0, 8), (1, 4)))
    first_coords = draw_first_coords(jax.random.fold_in(arg_keys[6], 71), 0)
    second_blocks = gaussian(arg_keys[4], (N_COL, N_ROW, CAP, BLK, BLK), (FF // 8) ** -0.5, 0.0625, ((0, 4), (1, 8)))
    second_coords = draw_second_coords(jax.random.fold_in(arg_keys[6], 71), 0)
    return dict(activations=activations, grad_out=grad_out, first_blocks=first_blocks, first_coords=first_coords, second_blocks=second_blocks, second_coords=second_coords)


def gelu_tanh(values):
    return jax.nn.gelu(values, approximate=True)

def tile_product(panels, blocks, coords, source_axis, target_axis, segments, flipped):
    token_count = panels.shape[0]
    block_grid = panels.reshape(token_count, -1, BLK)
    flat_blocks = blocks.reshape(-1, CAP, BLK, BLK)
    flat_coords = coords.reshape(-1, CAP, 2)

    def advance(totals, member):
        tile_blocks, tile_coords = member
        is_live = tile_coords[:, 0] >= 0
        source = jnp.where(is_live, tile_coords[:, source_axis], 0).astype(jnp.int32)
        target = jnp.where(is_live, tile_coords[:, target_axis], segments).astype(jnp.int32)
        picked = jnp.take(block_grid, source, axis=1).astype(jnp.float32)
        weights = tile_blocks.astype(jnp.float32)
        if flipped:
            products = jnp.einsum('rsk,snk->srn', picked, weights)
        else:
            products = jnp.einsum('rsk,skn->srn', picked, weights)
        return (totals.at[target].add(products), None)
    initial = jnp.zeros((segments + 1, token_count, BLK), jnp.float32)
    totals, unused = lax.scan(advance, initial, (flat_blocks, flat_coords))
    return jnp.transpose(totals[:segments], (1, 0, 2)).reshape(token_count, segments * BLK)

def tile_grads(left, right, coords, blocks_shape):
    token_count = left.shape[0]
    left_grid = left.reshape(token_count, -1, BLK)
    right_grid = right.reshape(token_count, -1, BLK)
    flat_coords = coords.reshape(-1, CAP, 2)

    def advance(carry, tile_coords):
        is_live = tile_coords[:, 0] >= 0
        left_source = jnp.where(is_live, tile_coords[:, 0], 0).astype(jnp.int32)
        right_source = jnp.where(is_live, tile_coords[:, 1], 0).astype(jnp.int32)
        picked_left = jnp.take(left_grid, left_source, axis=1).astype(jnp.float32)
        picked_right = jnp.take(right_grid, right_source, axis=1).astype(jnp.float32)
        grads = jnp.einsum('rsk,rsn->skn', picked_left, picked_right)
        grads = jnp.where(is_live[:, None, None], grads, jnp.float32(0.0)).astype(jnp.bfloat16)
        return (carry, grads)
    unused, stacked = lax.scan(advance, jnp.zeros((), jnp.float32), flat_coords)
    return stacked.reshape(blocks_shape)

def reference(activations, grad_out, first_blocks, first_coords, second_blocks, second_coords):
    pre = tile_product(activations, first_blocks, first_coords, 0, 1, FB, False)
    hidden_full, gelu_back = jax.vjp(gelu_tanh, pre)
    hidden = hidden_full.astype(jnp.bfloat16)
    output = tile_product(hidden, second_blocks, second_coords, 0, 1, DB, False)
    grad_hidden = tile_product(grad_out, second_blocks, second_coords, 1, 0, FB, True)
    grad_pre = gelu_back(grad_hidden)[0].astype(jnp.bfloat16)
    grad_input = tile_product(grad_pre, first_blocks, first_coords, 1, 0, DB, True)
    grad_first = tile_grads(activations, grad_pre, first_coords, first_blocks.shape)
    grad_second = tile_grads(hidden, grad_out, second_coords, second_blocks.shape)
    return (output, grad_input, grad_first, grad_second)
```

```python
import functools
import math

import jax
import jax.numpy as jnp
from jax import lax
from jax.experimental import pallas as pl
from jax.experimental.pallas import tpu as pltpu
from jax.sharding import PartitionSpec as P

FF = 65536
CHUNK = 32
VMEM_LIMIT = 58 * 1024 * 1024


def gelu_tanh(values):
    return jax.nn.gelu(values, approximate=True)


def contract(left, right, left_dim, right_dim):
    return lax.dot_general(
        left, right, (((left_dim,), (right_dim,)), ((), ())), preferred_element_type=jnp.float32
    )


def lanes(ref, index, width):
    return ref[:, pl.ds(pl.multiple_of(index * width, width), width)]


def to_hidden_kernel(flipped, source, target, panel, weights, keep, send, totals):
    step = pl.program_id(0)
    segments = totals.shape[0] - 1
    half = segments // 2
    width = weights.shape[-1]

    @pl.when(step == 0)
    def _():
        def clear(index, carry):
            totals[index] = jnp.zeros(totals.shape[1:], jnp.float32)
            return carry

        lax.fori_loop(0, segments, clear, 0)

    for slot in range(CHUNK):
        k = step * CHUNK + slot
        term = contract(
            lanes(panel, source[k], width), weights[slot], 1, 1 if flipped else 0
        )
        totals[target[k]] += term

    @pl.when(step == pl.num_programs(0) - 1)
    def _():
        def write(index, carry):
            keep[index] = totals[index]
            send[index] = totals[half + index].astype(jnp.bfloat16)
            return carry

        lax.fori_loop(0, half, write, 0)


def to_hidden(panel, weights, source, target, segments, flipped):
    tokens = panel.shape[0]
    slots, width, _ = weights.shape
    half = segments // 2
    return pl.pallas_call(
        functools.partial(to_hidden_kernel, flipped),
        grid_spec=pltpu.PrefetchScalarGridSpec(
            num_scalar_prefetch=2,
            grid=(slots // CHUNK,),
            in_specs=[
                pl.BlockSpec(panel.shape, lambda s, a, b: (0, 0)),
                pl.BlockSpec((CHUNK, width, width), lambda s, a, b: (s, 0, 0)),
            ],
            out_specs=[pl.BlockSpec((half, tokens, width), lambda s, a, b: (0, 0, 0))] * 2,
            scratch_shapes=[pltpu.VMEM((segments + 1, tokens, width), jnp.float32)],
        ),
        out_shape=[
            jax.ShapeDtypeStruct((half, tokens, width), jnp.float32),
            jax.ShapeDtypeStruct((half, tokens, width), jnp.bfloat16),
        ],
        compiler_params=pltpu.CompilerParams(vmem_limit_bytes=VMEM_LIMIT),
        cost_estimate=pl.CostEstimate(
            flops=8 * slots * tokens * width * width,
            bytes_accessed=2 * weights.size + 6 * half * tokens * width,
            transcendentals=0,
        ),
    )(source, target, panel, weights)


def fetch(parts, hidden, sems):
    copies = []
    start = 0
    for number, part in enumerate(parts):
        count = part.shape[0]
        copies.append(pltpu.make_async_copy(part, hidden.at[pl.ds(start, count)], sems.at[number]))
        copies[-1].start()
        start += count
    for copy in copies:
        copy.wait()


def to_model_kernel(transposed, pieces, with_sums, with_grads, model_at, hidden_at, live, *refs):
    refs = list(refs)
    panel = refs.pop(0) if with_grads else None
    weights = refs.pop(0) if with_sums else None
    hidden_parts = [refs.pop(0) for _ in range(pieces)]
    grads = refs.pop(0) if with_grads else None
    own, send, totals = [refs.pop(0) for _ in range(3)] if with_sums else (None, None, None)
    hidden, sems = refs
    step = pl.program_id(0)
    width = hidden.shape[-1]

    @pl.when(step == 0)
    def _():
        if with_sums:
            totals[...] = jnp.zeros(totals.shape, jnp.float32)
        fetch(hidden_parts, hidden, sems)

    for slot in range(CHUNK):
        k = step * CHUNK + slot
        model = model_at[k]
        values = hidden[hidden_at[k]]
        is_live = live[k] > 0
        if with_sums:
            term = contract(values, weights[slot], 1, 1 if transposed else 0)
            totals[jnp.where(is_live, model, totals.shape[0] - 1)] += term
        if with_grads:
            other = lanes(panel, model, width)
            if transposed:
                grad = contract(other, values, 0, 0)
            else:
                grad = contract(values, other, 0, 0)
            grads[slot] = jnp.where(is_live, grad, 0.0).astype(jnp.bfloat16)

    if with_sums:

        @pl.when(step == pl.num_programs(0) - 1)
        def _():
            share = own.shape[0]
            for segment in range(totals.shape[0] - 1):
                columns = pl.ds(segment * width, width)
                own[:, columns] = totals[segment, pl.ds(0, share), :]
                for number, piece in enumerate(send):
                    rows = pl.ds((number + 1) * share, share)
                    piece[:, columns] = totals[segment, rows, :].astype(jnp.bfloat16)


def to_model(
    panel, hidden_parts, weights, places, members, transposed, with_sums=True, with_grads=True
):
    tokens, columns = panel.shape
    slots, width, _ = weights.shape
    segments = columns // width
    share = tokens // members
    hidden_count = sum(part.shape[0] for part in hidden_parts)
    pieces = len(hidden_parts)
    chunk_spec = pl.BlockSpec((CHUNK, width, width), lambda s, a, b, c: (s, 0, 0))
    share_spec = pl.BlockSpec((share, columns), lambda s, a, b, c: (0, 0))
    operands, in_specs, out_specs, out_shape, scratch = [], [], [], [], []
    if with_grads:
        operands.append(panel)
        in_specs.append(pl.BlockSpec(panel.shape, lambda s, a, b, c: (0, 0)))
        out_specs.append(chunk_spec)
        out_shape.append(jax.ShapeDtypeStruct(weights.shape, jnp.bfloat16))
    if with_sums:
        operands.append(weights)
        in_specs.append(chunk_spec)
        out_specs += [share_spec, [share_spec] * (members - 1)]
        out_shape += [
            jax.ShapeDtypeStruct((share, columns), jnp.float32),
            [jax.ShapeDtypeStruct((share, columns), jnp.bfloat16)] * (members - 1),
        ]
        scratch.append(pltpu.VMEM((segments + 1, tokens, width), jnp.float32))
    scratch += [
        pltpu.VMEM((hidden_count, tokens, width), jnp.bfloat16),
        pltpu.SemaphoreType.DMA((pieces,)),
    ]

    def kernel(*refs):
        flat = list(refs)
        if with_sums:
            start = 3 + len(operands) + pieces + (1 if with_grads else 0) + 1
            if not isinstance(flat[start], (list, tuple)):
                flat[start : start + members - 1] = [flat[start : start + members - 1]]
        to_model_kernel(transposed, pieces, with_sums, with_grads, *flat)

    return pl.pallas_call(
        kernel,
        grid_spec=pltpu.PrefetchScalarGridSpec(
            num_scalar_prefetch=3,
            grid=(slots // CHUNK,),
            in_specs=in_specs + [pl.BlockSpec(memory_space=pl.ANY)] * pieces,
            out_specs=out_specs,
            scratch_shapes=scratch,
        ),
        out_shape=out_shape,
        compiler_params=pltpu.CompilerParams(vmem_limit_bytes=VMEM_LIMIT),
        cost_estimate=pl.CostEstimate(
            flops=8 * slots * tokens * width * width * (with_sums + with_grads),
            bytes_accessed=4 * weights.size + 2 * hidden_count * tokens * width,
            transcendentals=0,
        ),
    )(*places, *operands, *hidden_parts)


def swap(values, bit):
    count = lax.axis_size("row")
    return lax.ppermute(values, "row", [(s, s ^ (1 << bit)) for s in range(count)])


def swap_orders():
    rest = list(range(1, int(math.log2(lax.axis_size("row")))))
    return [rest, rest[::-1]]


def hidden_position(index, segments):
    level = int(math.log2(segments))
    row = lax.axis_index("row")
    masks = []
    for order in swap_orders():
        mask = (row & 1) << (level - 1)
        for number, bit in enumerate(order):
            mask = mask | (((row >> bit) & 1) << (level - 3 - number))
        masks.append(mask)
    is_late = ((index >> (level - 2)) & 1) > 0
    return index ^ jnp.where(is_late, masks[1], masks[0])


def after(values, *earlier):
    return lax.optimization_barrier((values, earlier))[0]


def added(terms, start, count):
    total = None
    for array, base in terms:
        piece = array[base + start : base + start + count].astype(jnp.float32)
        total = piece if total is None else total + piece
    return total


def scatter_begin(keep, send, *earlier):
    arrived = swap(send, 0)
    quarter = keep.shape[0] // 2
    half = quarter // 2
    parts = [[(keep, n * quarter), (arrived, n * quarter)] for n in range(2)]
    sent = [added(terms, half, half).astype(jnp.bfloat16) for terms in parts]
    outgoing = after(sent, *earlier) if earlier else sent
    return arrived, sent, [swap(v, order[0]) for v, order in zip(outgoing, swap_orders())]


GELU_SCALE = math.sqrt(2.0 / math.pi)


def gelu_and_slope(values):
    square = values * values
    bent = jnp.tanh(GELU_SCALE * (values + 0.044715 * (values * square)))
    half = 0.5 * (1.0 + bent)
    slope = half + (0.5 * GELU_SCALE) * values * (1.0 - bent * bent) * (
        1.0 + (3.0 * 0.044715) * square
    )
    return values * half, slope


def exchange_kernel(sizes, *refs):
    segments, quarter, own, bits = sizes
    refs = list(refs)
    pre_keep, pre_core, pre_first = refs[0], refs[1], refs[2:4]
    back_keep, back_send = refs[4:6]
    hidden, near, far = refs[6], refs[7:9], refs[9:11]
    (acc, core_in, first_in, back, back_in, stage_out, stage_in, own_hidden, own_back) = refs[11:20]
    local_sems, send_sems, recv_sems = refs[20:]
    half = quarter // 2
    row = lax.axis_index("row")
    orders = [list(range(1, bits)), list(range(1, bits))[::-1]]
    tokens = acc.shape[2]
    strip = 32
    started = []
    counts = [0, 0]

    def local(source, target):
        copy = pltpu.make_async_copy(source, target, local_sems.at[counts[0]])
        counts[0] += 1
        copy.start()
        return copy

    def remote(source, target, bit):
        partner = row ^ (1 << bit)
        copy = pltpu.make_async_remote_copy(
            src_ref=source,
            dst_ref=target,
            send_sem=send_sems.at[counts[1]],
            recv_sem=recv_sems.at[counts[1]],
            device_id={"row": partner},
            device_id_type=pl.DeviceIdType.MESH,
        )
        counts[1] += 1
        copy.start()
        started.append(copy)
        return copy

    def over(count, step):
        def blocks(index, carry):
            for start in range(0, tokens, strip):
                step(index, pl.ds(start, strip))
            return carry

        lax.fori_loop(0, count, blocks, 0)

    loads = []
    for n in range(2):
        whole = pl.ds(n * quarter, half)
        loads.append(
            [
                local(pre_keep.at[whole], acc.at[n]),
                local(pre_core.at[whole], core_in.at[n]),
                local(pre_first[n], first_in.at[n]),
            ]
        )
    back_loads = [local(back_keep.at[pl.ds(n * quarter, quarter)], back.at[n]) for n in range(2)]

    barrier = pltpu.get_barrier_semaphore()
    for bit in range(bits):
        pl.semaphore_signal(
            barrier,
            inc=1,
            device_id={"row": row ^ (1 << bit)},
            device_id_type=pl.DeviceIdType.MESH,
        )
    pl.semaphore_wait(barrier, bits)

    core_swaps = []
    for start in (half, 0):
        for n in range(2):
            core_swaps.append(
                remote(
                    back_send.at[pl.ds(n * quarter + start, half)],
                    back_in.at[n, pl.ds(start, half)],
                    0,
                )
            )

    offset = [0]

    def slot(count):
        offset[0] += count
        return offset[0] - count

    def stage_send(n, bit, count, value):
        base = slot(count)

        def step(index, rows):
            stage_out[base + index, rows] = value(index, rows).astype(jnp.bfloat16)

        over(count, step)
        copy = remote(stage_out.at[pl.ds(base, count)], stage_in.at[pl.ds(base, count)], bit)
        return copy, base

    def fold_front(n, count):
        def step(index, rows):
            acc[n, index, rows] = (
                acc[n, index, rows]
                + core_in[n, index, rows].astype(jnp.float32)
                + first_in[n, index, rows].astype(jnp.float32)
            )

        over(count, step)

    pre_flight = [None, None]
    count = half // 2
    for n in range(2):
        for copy in loads[n]:
            copy.wait()
        pre_flight[n] = stage_send(
            n,
            orders[n][1],
            count,
            lambda i, r, n=n: acc[n, count + i, r]
            + core_in[n, count + i, r].astype(jnp.float32)
            + first_in[n, count + i, r].astype(jnp.float32),
        )
    for n in range(2):
        fold_front(n, count)

    back_flight = [None, None]
    for n in range(2):
        back_loads[n].wait()
        core_swaps[n].wait_recv()
        back_flight[n] = stage_send(
            n,
            orders[n][0],
            half,
            lambda i, r, n=n: back[n, half + i, r] + back_in[n, half + i, r].astype(jnp.float32),
        )

    def settle(ref, n, flight, count, later):
        for bit in later:
            copy, base = flight
            copy.wait_recv()
            lower = count // 2

            def value(i, r):
                return ref[n, lower + i, r] + stage_in[base + lower + i, r].astype(jnp.float32)

            flight = stage_send(n, bit, lower, value)

            def fold(i, r):
                ref[n, i, r] = ref[n, i, r] + stage_in[base + i, r].astype(jnp.float32)

            over(lower, fold)
            count = lower
        return flight

    gathers = [None, None]
    kept = [None, None]
    for n in range(2):
        flight, base = settle(acc, n, pre_flight[n], count, orders[n][2:])
        flight.wait_recv()

        def act(i, r):
            value, slope = gelu_and_slope(
                acc[n, i, r] + stage_in[base + i, r].astype(jnp.float32)
            )
            own_hidden[n, i, r] = value.astype(jnp.bfloat16)
            acc[n, i, r] = slope

        over(own, act)
        start = n * quarter
        kept[n] = local(own_hidden.at[n], hidden.at[pl.ds(start, own)])
        gathers[n] = remote(
            own_hidden.at[n], hidden.at[pl.ds(start + own, own)], orders[n][-1]
        )

    for n in range(2):
        core_swaps[2 + n].wait_recv()

        def fold(i, r):
            back[n, i, r] = back[n, i, r] + back_in[n, i, r].astype(jnp.float32)

        over(half, fold)

    for n in range(2):
        flight, base = back_flight[n]
        back_flight[n] = settle(back, n, back_flight[n], half, orders[n][1:2])

    for n in range(2):
        start = n * quarter
        size = own
        kept[n].wait()
        for bit in orders[n][::-1][1:]:
            gathers[n].wait_recv()
            size = size * 2
            gathers[n] = remote(
                hidden.at[pl.ds(start, size)], hidden.at[pl.ds(start + size, size)], bit
            )
    far_copies = []
    for n in range(2):
        start = n * quarter
        far_copies.append(
            remote(
                hidden.at[pl.ds(start, half)], hidden.at[pl.ds(2 * quarter + start, half)], 0
            )
        )

    spread = [None, None]
    held = [None, None]
    for n in range(2):
        flight, base = settle(back, n, back_flight[n], half // 2, orders[n][2:])
        flight.wait_recv()

        def cotangent(i, r):
            value = back[n, i, r] + stage_in[base + i, r].astype(jnp.float32)
            own_back[n, i, r] = (value * acc[n, i, r]).astype(jnp.bfloat16)

        over(own, cotangent)
        held[n] = local(own_back.at[n], near[n].at[pl.ds(0, own)])
        spread[n] = remote(own_back.at[n], near[n].at[pl.ds(own, own)], orders[n][-1])

    for n in range(2):
        size = own
        held[n].wait()
        for bit in orders[n][::-1][1:-1]:
            spread[n].wait_recv()
            size = size * 2
            spread[n] = remote(near[n].at[pl.ds(0, size)], near[n].at[pl.ds(size, size)], bit)
        spread[n].wait_recv()
        far_copies.append(remote(near[n], far[n], 0))

    for n in range(2):
        gathers[n].wait_recv()
        start = n * quarter + half
        far_copies.append(
            remote(
                hidden.at[pl.ds(start, half)], hidden.at[pl.ds(2 * quarter + start, half)], 0
            )
        )
    for copy in far_copies:
        copy.wait_recv()
    for copy in started:
        copy.wait_send()


def exchange(pre_keep, pre_core, pre_first, back_keep, back_send):
    held, tokens, width = pre_keep.shape
    segments = 2 * held
    quarter = held // 2
    half = quarter // 2
    bits = int(math.log2(lax.axis_size("row")))
    own = quarter >> (bits - 1)
    staged = 2 * (half - own) + 2 * (quarter - own)
    copies = 4 + 2 * (bits - 2) + 2 * (bits - 1) + 2 * (bits - 1) + 2 * (bits - 2) + 6
    wide, narrow = jnp.float32, jnp.bfloat16

    def hbm(count):
        return jax.ShapeDtypeStruct((count, tokens, width), narrow)

    return pl.pallas_call(
        functools.partial(exchange_kernel, (segments, quarter, own, bits)),
        in_specs=[pl.BlockSpec(memory_space=pl.ANY)] * 6,
        out_specs=[pl.BlockSpec(memory_space=pl.ANY)] * 5,
        out_shape=[hbm(segments)] + [hbm(half)] * 4,
        scratch_shapes=[
            pltpu.VMEM((2, half, tokens, width), wide),
            pltpu.VMEM((2, half, tokens, width), narrow),
            pltpu.VMEM((2, half, tokens, width), narrow),
            pltpu.VMEM((2, quarter, tokens, width), wide),
            pltpu.VMEM((2, quarter, tokens, width), narrow),
            pltpu.VMEM((staged, tokens, width), narrow),
            pltpu.VMEM((staged, tokens, width), narrow),
            pltpu.VMEM((2, own, tokens, width), narrow),
            pltpu.VMEM((2, own, tokens, width), narrow),
            pltpu.SemaphoreType.DMA((12,)),
            pltpu.SemaphoreType.DMA((copies,)),
            pltpu.SemaphoreType.DMA((copies,)),
        ],
        compiler_params=pltpu.CompilerParams(
            collective_id=1, has_side_effects=True, vmem_limit_bytes=VMEM_LIMIT
        ),
        cost_estimate=pl.CostEstimate(
            flops=40 * segments * tokens * width,
            bytes_accessed=30 * segments * tokens * width // 2,
            transcendentals=2 * own * tokens * width,
        ),
    )(pre_keep, pre_core, *pre_first, back_keep, back_send)


RELAY_ROWS = 16


def relay_kernel(members, own_ref, all_ref, local_sem, send_sems, recv_sems):
    share = own_ref.shape[0]
    pieces = share // RELAY_ROWS
    me = lax.axis_index("col")
    hops = members - 1

    def place(block, device, piece):
        slot = (block - device + members) % members
        return pl.ds(pl.multiple_of(slot * share + piece * RELAY_ROWS, RELAY_ROWS), RELAY_ROWS)

    mine = pltpu.make_async_copy(own_ref, all_ref.at[pl.ds(0, share)], local_sem)
    mine.start()
    barrier = pltpu.get_barrier_semaphore()
    for step in (1, -1):
        inside = (me + step >= 0) & (me + step < members)

        @pl.when(inside)
        def _():
            pl.semaphore_signal(
                barrier,
                inc=1,
                device_id={"col": me + step},
                device_id_type=pl.DeviceIdType.MESH,
            )

    pl.semaphore_wait(barrier, jnp.where((me > 0) & (me < members - 1), 2, 1))

    def move(side, hop, piece):
        step = 1 if side == 0 else -1
        block = me - step * hop
        target = jnp.clip(me + step, 0, members - 1)
        block = jnp.clip(block, 0, members - 1)
        if hop == 0:
            source = own_ref.at[pl.ds(piece * RELAY_ROWS, RELAY_ROWS)]
        else:
            source = all_ref.at[place(block, me, piece)]
        at = (side * hops + hop) * pieces + piece
        return pltpu.make_async_remote_copy(
            src_ref=source,
            dst_ref=all_ref.at[place(block, target, piece)],
            send_sem=send_sems.at[at],
            recv_sem=recv_sems.at[at],
            device_id={"col": target},
            device_id_type=pl.DeviceIdType.MESH,
        )

    def exists(side, hop):
        step = 1 if side == 0 else -1
        block = me - step * hop
        target = me + step
        return (block >= 0) & (block < members) & (target >= 0) & (target < members)

    def comes(side, hop):
        step = 1 if side == 0 else -1
        block = me - step * (hop + 1)
        return (block >= 0) & (block < members)

    for hop in range(members):
        for piece in range(pieces):
            for side in range(2):
                if hop > 0:

                    @pl.when(comes(side, hop - 1))
                    def _():
                        move(side, hop - 1, piece).wait_recv()

                if hop < hops:

                    @pl.when(exists(side, hop))
                    def _():
                        move(side, hop, piece).start()

    for hop in range(hops):
        for piece in range(pieces):
            for side in range(2):

                @pl.when(exists(side, hop))
                def _():
                    move(side, hop, piece).wait_send()

    mine.wait()


def relay_tokens(values):
    members = lax.axis_size("col")
    share, columns = values.shape
    copies = 2 * (members - 1) * (share // RELAY_ROWS)
    return pl.pallas_call(
        functools.partial(relay_kernel, members),
        in_specs=[pl.BlockSpec(memory_space=pl.ANY)],
        out_specs=pl.BlockSpec(memory_space=pl.ANY),
        out_shape=jax.ShapeDtypeStruct((members * share, columns), values.dtype),
        scratch_shapes=[
            pltpu.SemaphoreType.DMA,
            pltpu.SemaphoreType.DMA((copies,)),
            pltpu.SemaphoreType.DMA((copies,)),
        ],
        compiler_params=pltpu.CompilerParams(collective_id=2, has_side_effects=True),
    )(values)


def shift(values, distance):
    count = lax.axis_size("col")
    return lax.ppermute(values, "col", [(s, (s + distance) % count) for s in range(count)])


def gather_tokens(values):
    count = lax.axis_size("col")
    return jnp.concatenate([values] + [shift(values, -d) for d in range(1, count)], axis=0)


def scatter_tokens(own, send):
    total = own
    for number, piece in enumerate(send):
        total = total + shift(piece, number + 1).astype(jnp.float32)
    return total


def body(activations, grad_out, first_blocks, first_coords, second_blocks, second_coords):
    width = first_blocks.shape[-1]
    members = lax.axis_size("col")
    row_tiles = activations.shape[1] // width
    col_tiles = FF // width // members
    row_base = lax.axis_index("row") * row_tiles
    col_base = lax.axis_index("col") * col_tiles

    def fields(model, hidden):
        is_live = model >= 0
        model_at = jnp.where(is_live, model - row_base, 0)
        hidden_at = jnp.where(is_live, hidden_position(hidden - col_base, col_tiles), 0)
        target = jnp.where(is_live, hidden_at, col_tiles)
        return model_at, hidden_at, target, is_live.astype(jnp.int32)

    model_one, hidden_one, target_one, live_one = fields(
        first_coords[0, 0, :, 0], first_coords[0, 0, :, 1]
    )
    model_two, hidden_two, target_two, live_two = fields(
        second_coords[0, 0, :, 1], second_coords[0, 0, :, 0]
    )
    weights_one = first_blocks[0, 0]
    weights_two = second_blocks[0, 0]

    inputs_all = relay_tokens(activations)
    cotangent_all = gather_tokens(after(grad_out, inputs_all))
    pre_keep, pre_send = to_hidden(
        inputs_all, weights_one, model_one, target_one, col_tiles, False
    )
    pre_core, pre_sent, pre_first = scatter_begin(pre_keep, after(pre_send, cotangent_all))
    back_keep, back_send = to_hidden(
        after(cotangent_all, *pre_sent), weights_two, model_two, target_two, col_tiles, True
    )
    hidden, near_a, near_b, far_a, far_b = exchange(
        pre_keep, pre_core, pre_first, back_keep, back_send
    )
    orders = swap_orders()
    last_a, last_b = swap(near_a, orders[0][0]), swap(near_b, orders[1][0])
    grad_second, own_out, send_out = to_model(
        cotangent_all, [hidden], weights_two, (model_two, hidden_two, live_two), members, False
    )
    far_last_a = swap(after(last_a, own_out), 0)
    far_last_b = swap(after(last_b, own_out), 0)
    grad_pre_parts = [near_a, last_a, near_b, last_b, far_a, far_last_a, far_b, far_last_b]
    output = scatter_tokens(own_out, after(send_out, *grad_pre_parts))
    places_one = (model_one, hidden_one, live_one)
    own_in, send_in = to_model(
        inputs_all,
        grad_pre_parts,
        weights_one,
        places_one,
        members,
        True,
        with_grads=False,
    )
    grad_input = scatter_tokens(own_in, send_in)
    (grad_first,) = to_model(
        inputs_all,
        after(grad_pre_parts, own_in, output),
        weights_one,
        places_one,
        members,
        True,
        with_sums=False,
    )
    return (output, grad_input, grad_first[None, None], grad_second[None, None])


def solution(mesh):
    return jax.shard_map(
        body,
        mesh=mesh,
        in_specs=(
            P("col", "row"),
            P("col", "row"),
            P("row", "col", None, None, None),
            P("row", "col", None, None),
            P("col", "row", None, None, None),
            P("col", "row", None, None),
        ),
        out_specs=(
            P("col", "row"),
            P("col", "row"),
            P("row", "col", None, None, None),
            P("col", "row", None, None, None),
        ),
        check_vma=False,
    )
```

```python
import functools
import math

import jax
import jax.numpy as jnp
from jax import lax
from jax.experimental import pallas as pl
from jax.experimental.pallas import tpu as pltpu
from jax.sharding import PartitionSpec as P

FF = 65536
CHUNK = 32
VMEM_LIMIT = 58 * 1024 * 1024


def gelu_tanh(values):
    return jax.nn.gelu(values, approximate=True)


def contract(left, right, left_dim, right_dim):
    return lax.dot_general(
        left, right, (((left_dim,), (right_dim,)), ((), ())), preferred_element_type=jnp.float32
    )


def lanes(ref, index, width):
    return ref[:, pl.ds(pl.multiple_of(index * width, width), width)]


def to_hidden_kernel(flipped, source, target, panel, weights, keep, send, totals):
    step = pl.program_id(0)
    segments = totals.shape[0] - 1
    half = segments // 2
    width = weights.shape[-1]

    @pl.when(step == 0)
    def _():
        def clear(index, carry):
            totals[index] = jnp.zeros(totals.shape[1:], jnp.float32)
            return carry

        lax.fori_loop(0, segments, clear, 0)

    for slot in range(CHUNK):
        k = step * CHUNK + slot
        term = contract(
            lanes(panel, source[k], width), weights[slot], 1, 1 if flipped else 0
        )
        totals[target[k]] += term

    @pl.when(step == pl.num_programs(0) - 1)
    def _():
        def write(index, carry):
            keep[index] = totals[index]
            send[index] = totals[half + index].astype(jnp.bfloat16)
            return carry

        lax.fori_loop(0, half, write, 0)


def to_hidden(panel, weights, source, target, segments, flipped):
    tokens = panel.shape[0]
    slots, width, _ = weights.shape
    half = segments // 2
    return pl.pallas_call(
        functools.partial(to_hidden_kernel, flipped),
        grid_spec=pltpu.PrefetchScalarGridSpec(
            num_scalar_prefetch=2,
            grid=(slots // CHUNK,),
            in_specs=[
                pl.BlockSpec(panel.shape, lambda s, a, b: (0, 0)),
                pl.BlockSpec((CHUNK, width, width), lambda s, a, b: (s, 0, 0)),
            ],
            out_specs=[pl.BlockSpec((half, tokens, width), lambda s, a, b: (0, 0, 0))] * 2,
            scratch_shapes=[pltpu.VMEM((segments + 1, tokens, width), jnp.float32)],
        ),
        out_shape=[
            jax.ShapeDtypeStruct((half, tokens, width), jnp.float32),
            jax.ShapeDtypeStruct((half, tokens, width), jnp.bfloat16),
        ],
        compiler_params=pltpu.CompilerParams(vmem_limit_bytes=VMEM_LIMIT),
        cost_estimate=pl.CostEstimate(
            flops=8 * slots * tokens * width * width,
            bytes_accessed=2 * weights.size + 6 * half * tokens * width,
            transcendentals=0,
        ),
    )(source, target, panel, weights)


def fetch(parts, hidden, sems):
    copies = []
    start = 0
    for number, part in enumerate(parts):
        count = part.shape[0]
        copies.append(pltpu.make_async_copy(part, hidden.at[pl.ds(start, count)], sems.at[number]))
        copies[-1].start()
        start += count
    for copy in copies:
        copy.wait()


def to_model_kernel(transposed, pieces, with_sums, with_grads, model_at, hidden_at, live, *refs):
    refs = list(refs)
    panel = refs.pop(0) if with_grads else None
    weights = refs.pop(0) if with_sums else None
    hidden_parts = [refs.pop(0) for _ in range(pieces)]
    grads = refs.pop(0) if with_grads else None
    own, send, totals = [refs.pop(0) for _ in range(3)] if with_sums else (None, None, None)
    hidden, sems = refs
    step = pl.program_id(0)
    width = hidden.shape[-1]

    @pl.when(step == 0)
    def _():
        if with_sums:
            totals[...] = jnp.zeros(totals.shape, jnp.float32)
        fetch(hidden_parts, hidden, sems)

    for slot in range(CHUNK):
        k = step * CHUNK + slot
        model = model_at[k]
        values = hidden[hidden_at[k]]
        is_live = live[k] > 0
        if with_sums:
            term = contract(values, weights[slot], 1, 1 if transposed else 0)
            totals[jnp.where(is_live, model, totals.shape[0] - 1)] += term
        if with_grads:
            other = lanes(panel, model, width)
            if transposed:
                grad = contract(other, values, 0, 0)
            else:
                grad = contract(values, other, 0, 0)
            grads[slot] = jnp.where(is_live, grad, 0.0).astype(jnp.bfloat16)

    if with_sums:

        @pl.when(step == pl.num_programs(0) - 1)
        def _():
            share = own.shape[0]
            for segment in range(totals.shape[0] - 1):
                columns = pl.ds(segment * width, width)
                own[:, columns] = totals[segment, pl.ds(0, share), :]
                for number, piece in enumerate(send):
                    rows = pl.ds((number + 1) * share, share)
                    piece[:, columns] = totals[segment, rows, :].astype(jnp.bfloat16)


def to_model(
    panel, hidden_parts, weights, places, members, transposed, with_sums=True, with_grads=True
):
    tokens, columns = panel.shape
    slots, width, _ = weights.shape
    segments = columns // width
    share = tokens // members
    hidden_count = sum(part.shape[0] for part in hidden_parts)
    pieces = len(hidden_parts)
    chunk_spec = pl.BlockSpec((CHUNK, width, width), lambda s, a, b, c: (s, 0, 0))
    share_spec = pl.BlockSpec((share, columns), lambda s, a, b, c: (0, 0))
    operands, in_specs, out_specs, out_shape, scratch = [], [], [], [], []
    if with_grads:
        operands.append(panel)
        in_specs.append(pl.BlockSpec(panel.shape, lambda s, a, b, c: (0, 0)))
        out_specs.append(chunk_spec)
        out_shape.append(jax.ShapeDtypeStruct(weights.shape, jnp.bfloat16))
    if with_sums:
        operands.append(weights)
        in_specs.append(chunk_spec)
        out_specs += [share_spec, [share_spec] * (members - 1)]
        out_shape += [
            jax.ShapeDtypeStruct((share, columns), jnp.float32),
            [jax.ShapeDtypeStruct((share, columns), jnp.bfloat16)] * (members - 1),
        ]
        scratch.append(pltpu.VMEM((segments + 1, tokens, width), jnp.float32))
    scratch += [
        pltpu.VMEM((hidden_count, tokens, width), jnp.bfloat16),
        pltpu.SemaphoreType.DMA((pieces,)),
    ]

    def kernel(*refs):
        flat = list(refs)
        if with_sums:
            start = 3 + len(operands) + pieces + (1 if with_grads else 0) + 1
            if not isinstance(flat[start], (list, tuple)):
                flat[start : start + members - 1] = [flat[start : start + members - 1]]
        to_model_kernel(transposed, pieces, with_sums, with_grads, *flat)

    return pl.pallas_call(
        kernel,
        grid_spec=pltpu.PrefetchScalarGridSpec(
            num_scalar_prefetch=3,
            grid=(slots // CHUNK,),
            in_specs=in_specs + [pl.BlockSpec(memory_space=pl.ANY)] * pieces,
            out_specs=out_specs,
            scratch_shapes=scratch,
        ),
        out_shape=out_shape,
        compiler_params=pltpu.CompilerParams(vmem_limit_bytes=VMEM_LIMIT),
        cost_estimate=pl.CostEstimate(
            flops=8 * slots * tokens * width * width * (with_sums + with_grads),
            bytes_accessed=4 * weights.size + 2 * hidden_count * tokens * width,
            transcendentals=0,
        ),
    )(*places, *operands, *hidden_parts)


def swap(values, bit):
    count = lax.axis_size("row")
    return lax.ppermute(values, "row", [(s, s ^ (1 << bit)) for s in range(count)])


def swap_orders():
    rest = list(range(1, int(math.log2(lax.axis_size("row")))))
    return [rest, rest[::-1]]


def hidden_position(index, segments):
    level = int(math.log2(segments))
    row = lax.axis_index("row")
    masks = []
    for order in swap_orders():
        mask = (row & 1) << (level - 1)
        for number, bit in enumerate(order):
            mask = mask | (((row >> bit) & 1) << (level - 3 - number))
        masks.append(mask)
    is_late = ((index >> (level - 2)) & 1) > 0
    return index ^ jnp.where(is_late, masks[1], masks[0])


def after(values, *earlier):
    return lax.optimization_barrier((values, earlier))[0]


def added(terms, start, count):
    total = None
    for array, base in terms:
        piece = array[base + start : base + start + count].astype(jnp.float32)
        total = piece if total is None else total + piece
    return total


GELU_SCALE = math.sqrt(2.0 / math.pi)


def gelu_and_slope(values):
    square = values * values
    bent = jnp.tanh(GELU_SCALE * (values + 0.044715 * (values * square)))
    half = 0.5 * (1.0 + bent)
    slope = half + (0.5 * GELU_SCALE) * values * (1.0 - bent * bent) * (
        1.0 + (3.0 * 0.044715) * square
    )
    return values * half, slope


GROUP = 32
AHEAD = 3


def exchange_kernel(sizes, *refs):
    quarter, own, bits, members = sizes
    refs = list(refs)
    source_at, carries, ends, filled = refs[0:4]
    pre_keep, pre_send, cotangent, weights = refs[4:8]
    hidden, near, far, cotangent_out = refs[8], refs[9:11], refs[11:13], refs[13]
    (acc, core_in, back, back_in, stage_out, stage_in, own_hidden, own_back) = refs[14:22]
    (panel, tiles, blocks, running, sums) = refs[22:27]
    local_sems, block_sems, send_sems, recv_sems = refs[27:]
    half = quarter // 2
    row = lax.axis_index("row")
    col = lax.axis_index("col")
    orders = [list(range(1, bits)), list(range(1, bits))[::-1]]
    tokens, width = acc.shape[2:]
    share = tokens // members
    slots = weights.shape[0]
    groups = slots // GROUP
    strip = 32
    started = []
    counts = [0, 0]

    def local(source, target):
        copy = pltpu.make_async_copy(source, target, local_sems.at[counts[0]])
        counts[0] += 1
        copy.start()
        return copy

    def remote_to(source, target, device):
        copy = pltpu.make_async_remote_copy(
            src_ref=source,
            dst_ref=target,
            send_sem=send_sems.at[counts[1]],
            recv_sem=recv_sems.at[counts[1]],
            device_id=device,
            device_id_type=pl.DeviceIdType.MESH,
        )
        counts[1] += 1
        copy.start()
        started.append(copy)
        return copy

    def remote(source, target, bit):
        return remote_to(source, target, {"row": row ^ (1 << bit)})

    def over(count, step):
        def each(index, carry):
            for start in range(0, tokens, strip):
                step(index, pl.ds(start, strip))
            return carry

        lax.fori_loop(0, count, each, 0)

    def fetch_group(group):
        place = lax.rem(group, AHEAD)
        return pltpu.make_async_copy(
            weights.at[pl.ds(group * GROUP, GROUP)], blocks.at[place], block_sems.at[place]
        )

    loads = [local(pre_keep.at[pl.ds(n * quarter + half, half)], acc.at[n]) for n in range(2)]
    own_tokens = local(cotangent, panel.at[pl.ds(0, share)])
    for group in range(min(AHEAD, groups)):
        fetch_group(group).start()

    barrier = pltpu.get_barrier_semaphore()
    for bit in range(bits):
        pl.semaphore_signal(
            barrier,
            inc=1,
            device_id={"row": row ^ (1 << bit)},
            device_id_type=pl.DeviceIdType.MESH,
        )
    for distance in range(1, members):
        pl.semaphore_signal(
            barrier,
            inc=1,
            device_id={"col": lax.rem(col + distance, members)},
            device_id_type=pl.DeviceIdType.MESH,
        )
    pl.semaphore_wait(barrier, bits + members - 1)

    low = half // 2
    spans = ((half + low, low), (half, low), (0, half))

    def swap_core(n, span, source, target):
        return remote(source, target.at[n, pl.ds(*span)], 0)

    pre_core = [[], []]
    for span in spans:
        for n in range(2):
            source = pre_send.at[pl.ds(n * quarter + span[0], span[1])]
            pre_core[n].append(swap_core(n, span, source, core_in))
    arrivals = []
    for distance in range(1, members):
        slot = pl.ds((members - distance) * share, share)
        device = {"col": lax.rem(col + distance, members)}
        arrivals.append(remote_to(cotangent, panel.at[slot], device))

    pre_stages = []
    out_places = [0]
    in_places = [0]

    def stage_send(n, bit, count, value, ready):
        base, there = out_places[0], in_places[0]
        out_places[0] += count
        in_places[0] += count
        cut = count // 2
        copies = []
        for number, (start, size) in enumerate(((cut, count - cut), (0, cut))):
            ready[number]()

            def step(index, rows):
                stage_out[base + start + index, rows] = value(start + index, rows).astype(
                    jnp.bfloat16
                )

            over(size, step)
            copies.append(
                remote(
                    stage_out.at[pl.ds(base + start, size)],
                    stage_in.at[pl.ds(there + start, size)],
                    bit,
                )
            )
        pre_stages.append((copies, there))
        return copies, there

    def nothing():
        return None

    def arrived_at(base):
        return lambda i, r: stage_in[base + i, r].astype(jnp.float32)

    def pass_on(ref, n, flight, count, bit):
        copies, base = flight
        lower = count // 2
        copies[0].wait_recv()
        term = arrived_at(base)
        return stage_send(
            n,
            bit,
            lower,
            lambda i, r: ref[n, lower + i, r] + term(lower + i, r),
            (nothing, nothing),
        )

    def fold(ref, n, count, term):
        def step(i, r):
            ref[n, i, r] = ref[n, i, r] + term(i, r)

        over(count, step)

    def fold_rest(ref, n, flight, count):
        copies, base = flight
        copies[1].wait_recv()
        fold(ref, n, count // 2, arrived_at(base))

    def product(group, carry):
        fetch_group(group).wait()
        place = lax.rem(group, AHEAD)
        total = running[...]
        for slot in range(GROUP):
            k = group * GROUP + slot
            term = contract(tiles[source_at[k]], blocks[place, slot], 1, 1)
            total = total * carries[k] + term
            sums[k] = total.astype(jnp.bfloat16)
        running[...] = total

        @pl.when(group + AHEAD < groups)
        def _():
            fetch_group(group + AHEAD).start()

        return carry

    def summed(position, rows):
        return sums[ends[position], rows].astype(jnp.float32) * filled[position]

    def spread(target, n, stages, source, start, size, at, landed, number):
        for later in range(number, len(stages)):
            place = at + start + (own << later)
            copy = remote(source, target.at[pl.ds(place, size)], stages[later])
            landed[later].append((start + (own << later), size, copy))

    def forward(target, n, stages, at, landed, number):
        for start, size, copy in landed[number]:
            copy.wait_recv()
            piece = target.at[pl.ds(at + start, size)]
            spread(target, n, stages, piece, start, size, at, landed, number + 1)

    def cross(source, target, at, start, size):
        far_copies.append(remote(source, target.at[pl.ds(at + start, size)], 0))

    far_copies = []
    to_hidden_stages = [order[::-1] for order in orders]
    to_near_stages = [order[::-1][:-1] for order in orders]
    hidden_landed = [[[] for _ in stages] for stages in to_hidden_stages]
    near_landed = [[[] for _ in stages] for stages in to_near_stages]
    cut = own // 2
    own_spans = ((cut, own - cut), (0, cut))

    pre_flight = [None, None]
    for n in range(2):
        loads[n].wait()
        pre_flight[n] = stage_send(
            n,
            orders[n][0],
            half,
            lambda i, r, n=n: acc[n, i, r] + core_in[n, half + i, r].astype(jnp.float32),
            (pre_core[n][0].wait_recv, pre_core[n][1].wait_recv),
        )
        loads[n] = local(pre_keep.at[pl.ds(n * quarter, half)], acc.at[n])
    for n in range(2):
        loads[n].wait()
        pre_core[n][2].wait_recv()
        fold(acc, n, half, lambda i, r: core_in[n, i, r].astype(jnp.float32))
    running[...] = jnp.zeros(running.shape, jnp.float32)

    count = half
    marks = [0, groups // 3, 2 * groups // 3, groups]
    for number, _ in enumerate(orders[0][1:]):
        flights = [
            pass_on(acc, n, pre_flight[n], count, orders[n][1 + number]) for n in range(2)
        ]
        if number == 0:
            own_tokens.wait()
            for copy in arrivals:
                copy.wait_recv()
            given = local(panel, cotangent_out)
            for tile in range(tiles.shape[0]):
                tiles[tile] = panel[:, tile * width : (tile + 1) * width]
            lax.fori_loop(marks[0], marks[1], product, 0)
        for n in range(2):
            fold_rest(acc, n, pre_flight[n], count)
        pre_flight = flights
        count = count // 2
    lax.fori_loop(marks[1], marks[2], product, 0)

    kept = []
    for number, (start, size) in enumerate(own_spans):
        for n in range(2):
            copies, base = pre_flight[n]
            copies[number].wait_recv()

            def act(index, r):
                i = start + index
                value, slope = gelu_and_slope(
                    acc[n, i, r] + stage_in[base + i, r].astype(jnp.float32)
                )
                own_hidden[n, i, r] = value.astype(jnp.bfloat16)
                acc[n, i, r] = slope

            over(size, act)
            piece = own_hidden.at[n, pl.ds(start, size)]
            at = n * quarter
            spread(
                hidden, n, to_hidden_stages[n], piece, start, size, at, hidden_landed[n], 0
            )
            cross(piece, hidden, 2 * quarter + at, start, size)
            kept.append(local(piece, hidden.at[pl.ds(at + start, size)]))
        if number == 0:
            lax.fori_loop(marks[2], marks[3], product, 0)

    for copies, _ in pre_stages:
        for copy in copies:
            copy.wait_send()
            started[:] = [other for other in started if other is not copy]
    out_places[0] = 0
    back_core = [[], []]
    for first, size in spans:
        for n in range(2):

            def step(i, r):
                value = summed(2 * quarter + n * quarter + first + i, r)
                core_in[n, first + i, r] = value.astype(jnp.bfloat16)

            over(size, step)
            source = core_in.at[n, pl.ds(first, size)]
            back_core[n].append(swap_core(n, (first, size), source, back_in))
    back_flight = [None, None]
    for n in range(2):
        back_flight[n] = stage_send(
            n,
            orders[n][0],
            half,
            lambda i, r, n=n: summed(n * quarter + half + i, r)
            + back_in[n, half + i, r].astype(jnp.float32),
            (back_core[n][0].wait_recv, back_core[n][1].wait_recv),
        )
    for n in range(2):
        forward(hidden, n, to_hidden_stages[n], n * quarter, hidden_landed[n], 0)
    for n in range(2):
        back_core[n][2].wait_recv()

        def begin(i, r):
            back[n, i, r] = summed(n * quarter + i, r) + back_in[
                n, i, r
            ].astype(jnp.float32)

        over(half, begin)

    def cross_landed(target, other, n, at, there, landed, number):
        for start, size, copy in landed[number]:
            cross(target.at[pl.ds(at + start, size)], other, there, start, size)

    for n in range(2):
        at = n * quarter
        cross_landed(hidden, hidden, n, at, 2 * quarter + at, hidden_landed[n], 0)

    count = half
    for number, _ in enumerate(orders[0][1:]):
        flights = [
            pass_on(back, n, back_flight[n], count, orders[n][1 + number]) for n in range(2)
        ]
        for n in range(2):
            fold_rest(back, n, back_flight[n], count)
        back_flight = flights
        count = count // 2

    for number, (start, size) in enumerate(own_spans):
        for n in range(2):
            copies, base = back_flight[n]
            copies[number].wait_recv()

            def slope_times(index, r):
                i = start + index
                value = back[n, i, r] + stage_in[base + i, r].astype(jnp.float32)
                own_back[n, i, r] = (value * acc[n, i, r]).astype(jnp.bfloat16)

            over(size, slope_times)
            piece = own_back.at[n, pl.ds(start, size)]
            spread(near[n], n, to_near_stages[n], piece, start, size, 0, near_landed[n], 0)
            cross(piece, far[n], 0, start, size)
            kept.append(local(piece, near[n].at[pl.ds(start, size)]))

    for number in range(1, len(to_hidden_stages[0])):
        for n in range(2):
            at = n * quarter
            forward(hidden, n, to_hidden_stages[n], at, hidden_landed[n], number)
            cross_landed(hidden, hidden, n, at, 2 * quarter + at, hidden_landed[n], number)
    for number in range(len(to_near_stages[0])):
        for n in range(2):
            forward(near[n], n, to_near_stages[n], 0, near_landed[n], number)
            cross_landed(near[n], far[n], n, 0, 0, near_landed[n], number)
    given.wait()
    for copy in kept:
        copy.wait()
    for copy in far_copies:
        copy.wait_recv()
    for copy in started:
        copy.wait_send()


def exchange(pre_keep, pre_send, cotangent, weights, source_at, carries, ends, filled):
    held, tokens, width = pre_keep.shape
    columns = cotangent.shape[1]
    slots = weights.shape[0]
    segments = 2 * held
    quarter = held // 2
    half = quarter // 2
    bits = int(math.log2(lax.axis_size("row")))
    members = lax.axis_size("col")
    own = quarter >> (bits - 1)
    staged = 2 * (quarter - own)
    copies = members - 1 + 12 + 8 * (bits - 1) + 16 * (quarter // own)
    wide, narrow = jnp.float32, jnp.bfloat16

    def hbm(count):
        return jax.ShapeDtypeStruct((count, tokens, width), narrow)

    return pl.pallas_call(
        functools.partial(exchange_kernel, (quarter, own, bits, members)),
        in_specs=[pl.BlockSpec(memory_space=pltpu.SMEM)] * 4
        + [pl.BlockSpec(memory_space=pl.ANY)] * 4,
        out_specs=[pl.BlockSpec(memory_space=pl.ANY)] * 6,
        out_shape=[hbm(segments)]
        + [hbm(half)] * 4
        + [jax.ShapeDtypeStruct((tokens, columns), narrow)],
        scratch_shapes=[
            pltpu.VMEM((2, half, tokens, width), wide),
            pltpu.VMEM((2, quarter, tokens, width), narrow),
            pltpu.VMEM((2, half, tokens, width), wide),
            pltpu.VMEM((2, quarter, tokens, width), narrow),
            pltpu.VMEM((staged, tokens, width), narrow),
            pltpu.VMEM((2 * staged, tokens, width), narrow),
            pltpu.VMEM((2, own, tokens, width), narrow),
            pltpu.VMEM((2, own, tokens, width), narrow),
            pltpu.VMEM((tokens, columns), narrow),
            pltpu.VMEM((columns // width, tokens, width), narrow),
            pltpu.VMEM((AHEAD, GROUP, width, width), narrow),
            pltpu.VMEM((tokens, width), wide),
            pltpu.VMEM((slots, tokens, width), narrow),
            pltpu.SemaphoreType.DMA((16,)),
            pltpu.SemaphoreType.DMA((AHEAD,)),
            pltpu.SemaphoreType.DMA((copies,)),
            pltpu.SemaphoreType.DMA((copies,)),
        ],
        compiler_params=pltpu.CompilerParams(
            collective_id=1, has_side_effects=True, vmem_limit_bytes=VMEM_LIMIT
        ),
        cost_estimate=pl.CostEstimate(
            flops=8 * slots * tokens * width * width,
            bytes_accessed=30 * segments * tokens * width // 2,
            transcendentals=2 * own * tokens * width,
        ),
    )(source_at, carries, ends, filled, pre_keep, pre_send, cotangent, weights)


RELAY_ROWS = 16


def relay_kernel(members, own_ref, all_ref, local_sem, send_sems, recv_sems):
    share = own_ref.shape[0]
    pieces = share // RELAY_ROWS
    me = lax.axis_index("col")
    hops = members - 1

    def place(block, device, piece):
        slot = (block - device + members) % members
        return pl.ds(pl.multiple_of(slot * share + piece * RELAY_ROWS, RELAY_ROWS), RELAY_ROWS)

    mine = pltpu.make_async_copy(own_ref, all_ref.at[pl.ds(0, share)], local_sem)
    mine.start()
    barrier = pltpu.get_barrier_semaphore()
    for step in (1, -1):
        inside = (me + step >= 0) & (me + step < members)

        @pl.when(inside)
        def _():
            pl.semaphore_signal(
                barrier,
                inc=1,
                device_id={"col": me + step},
                device_id_type=pl.DeviceIdType.MESH,
            )

    pl.semaphore_wait(barrier, jnp.where((me > 0) & (me < members - 1), 2, 1))

    def move(side, hop, piece):
        step = 1 if side == 0 else -1
        block = me - step * hop
        target = jnp.clip(me + step, 0, members - 1)
        block = jnp.clip(block, 0, members - 1)
        if hop == 0:
            source = own_ref.at[pl.ds(piece * RELAY_ROWS, RELAY_ROWS)]
        else:
            source = all_ref.at[place(block, me, piece)]
        at = (side * hops + hop) * pieces + piece
        return pltpu.make_async_remote_copy(
            src_ref=source,
            dst_ref=all_ref.at[place(block, target, piece)],
            send_sem=send_sems.at[at],
            recv_sem=recv_sems.at[at],
            device_id={"col": target},
            device_id_type=pl.DeviceIdType.MESH,
        )

    def exists(side, hop):
        step = 1 if side == 0 else -1
        block = me - step * hop
        target = me + step
        return (block >= 0) & (block < members) & (target >= 0) & (target < members)

    def comes(side, hop):
        step = 1 if side == 0 else -1
        block = me - step * (hop + 1)
        return (block >= 0) & (block < members)

    for hop in range(members):
        for piece in range(pieces):
            for side in range(2):
                if hop > 0:

                    @pl.when(comes(side, hop - 1))
                    def _():
                        move(side, hop - 1, piece).wait_recv()

                if hop < hops:

                    @pl.when(exists(side, hop))
                    def _():
                        move(side, hop, piece).start()

    for hop in range(hops):
        for piece in range(pieces):
            for side in range(2):

                @pl.when(exists(side, hop))
                def _():
                    move(side, hop, piece).wait_send()

    mine.wait()


def relay_tokens(values):
    members = lax.axis_size("col")
    share, columns = values.shape
    copies = 2 * (members - 1) * (share // RELAY_ROWS)
    return pl.pallas_call(
        functools.partial(relay_kernel, members),
        in_specs=[pl.BlockSpec(memory_space=pl.ANY)],
        out_specs=pl.BlockSpec(memory_space=pl.ANY),
        out_shape=jax.ShapeDtypeStruct((members * share, columns), values.dtype),
        scratch_shapes=[
            pltpu.SemaphoreType.DMA,
            pltpu.SemaphoreType.DMA((copies,)),
            pltpu.SemaphoreType.DMA((copies,)),
        ],
        compiler_params=pltpu.CompilerParams(collective_id=2, has_side_effects=True),
    )(values)


def shift(values, distance):
    count = lax.axis_size("col")
    return lax.ppermute(values, "col", [(s, (s + distance) % count) for s in range(count)])


def gather_tokens(values):
    count = lax.axis_size("col")
    return jnp.concatenate([values] + [shift(values, -d) for d in range(1, count)], axis=0)


def scatter_tokens(own, send):
    total = own
    for number, piece in enumerate(send):
        total = total + shift(piece, number + 1).astype(jnp.float32)
    return total


def body(activations, grad_out, first_blocks, first_coords, second_blocks, second_coords):
    width = first_blocks.shape[-1]
    members = lax.axis_size("col")
    row_tiles = activations.shape[1] // width
    col_tiles = FF // width // members
    row_base = lax.axis_index("row") * row_tiles
    col_base = lax.axis_index("col") * col_tiles

    def fields(model, hidden):
        is_live = model >= 0
        model_at = jnp.where(is_live, model - row_base, 0)
        hidden_at = jnp.where(is_live, hidden_position(hidden - col_base, col_tiles), 0)
        target = jnp.where(is_live, hidden_at, col_tiles)
        return model_at, hidden_at, target, is_live.astype(jnp.int32)

    model_one, hidden_one, target_one, live_one = fields(
        first_coords[0, 0, :, 0], first_coords[0, 0, :, 1]
    )
    model_two, hidden_two, target_two, live_two = fields(
        second_coords[0, 0, :, 1], second_coords[0, 0, :, 0]
    )
    weights_one = first_blocks[0, 0]
    weights_two = second_blocks[0, 0]

    inputs_all = relay_tokens(activations)
    pre_keep, pre_send = to_hidden(
        inputs_all, weights_one, model_one, target_one, col_tiles, False
    )
    same = (target_two[1:] == target_two[:-1]).astype(jnp.float32)
    carries = jnp.concatenate([jnp.zeros((1,), jnp.float32), same])
    numbers = jnp.arange(target_two.shape[0], dtype=jnp.int32)
    places = jnp.arange(col_tiles, dtype=jnp.int32)
    lasts = jnp.max(
        jnp.where(target_two[None, :] == places[:, None], numbers[None, :], -1), axis=1
    )
    ends = jnp.maximum(lasts, 0)
    filled = (lasts >= 0).astype(jnp.float32)
    hidden, near_a, near_b, far_a, far_b, cotangent_all = exchange(
        pre_keep, pre_send, grad_out, weights_two, model_two, carries, ends, filled
    )
    orders = swap_orders()
    last_a, last_b = swap(near_a, orders[0][0]), swap(near_b, orders[1][0])
    grad_second, own_out, send_out = to_model(
        cotangent_all, [hidden], weights_two, (model_two, hidden_two, live_two), members, False
    )
    far_last_a = swap(after(last_a, own_out), 0)
    far_last_b = swap(after(last_b, own_out), 0)
    grad_pre_parts = [near_a, last_a, near_b, last_b, far_a, far_last_a, far_b, far_last_b]
    output = scatter_tokens(own_out, after(send_out, *grad_pre_parts))
    places_one = (model_one, hidden_one, live_one)
    own_in, send_in = to_model(
        inputs_all,
        grad_pre_parts,
        weights_one,
        places_one,
        members,
        True,
        with_grads=False,
    )
    grad_input = scatter_tokens(own_in, send_in)
    (grad_first,) = to_model(
        inputs_all,
        after(grad_pre_parts, own_in, output),
        weights_one,
        places_one,
        members,
        True,
        with_sums=False,
    )
    return (output, grad_input, grad_first[None, None], grad_second[None, None])


def solution(mesh):
    return jax.shard_map(
        body,
        mesh=mesh,
        in_specs=(
            P("col", "row"),
            P("col", "row"),
            P("row", "col", None, None, None),
            P("row", "col", None, None),
            P("col", "row", None, None, None),
            P("col", "row", None, None),
        ),
        out_specs=(
            P("col", "row"),
            P("col", "row"),
            P("row", "col", None, None, None),
            P("col", "row", None, None, None),
        ),
        check_vma=False,
    )
```

```python
import functools
import math

import jax
import jax.numpy as jnp
from jax import lax
from jax.experimental import pallas as pl
from jax.experimental.pallas import tpu as pltpu
from jax.sharding import PartitionSpec as P

FF = 65536
CHUNK = 32
VMEM_LIMIT = 58 * 1024 * 1024


def gelu_tanh(values):
    return jax.nn.gelu(values, approximate=True)


def contract(left, right, left_dim, right_dim):
    return lax.dot_general(
        left, right, (((left_dim,), (right_dim,)), ((), ())), preferred_element_type=jnp.float32
    )


def lanes(ref, index, width):
    return ref[:, pl.ds(pl.multiple_of(index * width, width), width)]


def to_hidden_kernel(flipped, source, target, panel, weights, keep, send, totals):
    step = pl.program_id(0)
    segments = totals.shape[0] - 1
    half = segments // 2
    width = weights.shape[-1]

    @pl.when(step == 0)
    def _():
        def clear(index, carry):
            totals[index] = jnp.zeros(totals.shape[1:], jnp.float32)
            return carry

        lax.fori_loop(0, segments, clear, 0)

    for slot in range(CHUNK):
        k = step * CHUNK + slot
        term = contract(
            lanes(panel, source[k], width), weights[slot], 1, 1 if flipped else 0
        )
        totals[target[k]] += term

    @pl.when(step == pl.num_programs(0) - 1)
    def _():
        def write(index, carry):
            keep[index] = totals[index]
            send[index] = totals[half + index].astype(jnp.bfloat16)
            return carry

        lax.fori_loop(0, half, write, 0)


def to_hidden(panel, weights, source, target, segments, flipped):
    tokens = panel.shape[0]
    slots, width, _ = weights.shape
    half = segments // 2
    return pl.pallas_call(
        functools.partial(to_hidden_kernel, flipped),
        grid_spec=pltpu.PrefetchScalarGridSpec(
            num_scalar_prefetch=2,
            grid=(slots // CHUNK,),
            in_specs=[
                pl.BlockSpec(panel.shape, lambda s, a, b: (0, 0)),
                pl.BlockSpec((CHUNK, width, width), lambda s, a, b: (s, 0, 0)),
            ],
            out_specs=[pl.BlockSpec((half, tokens, width), lambda s, a, b: (0, 0, 0))] * 2,
            scratch_shapes=[pltpu.VMEM((segments + 1, tokens, width), jnp.float32)],
        ),
        out_shape=[
            jax.ShapeDtypeStruct((half, tokens, width), jnp.float32),
            jax.ShapeDtypeStruct((half, tokens, width), jnp.bfloat16),
        ],
        compiler_params=pltpu.CompilerParams(vmem_limit_bytes=VMEM_LIMIT),
        cost_estimate=pl.CostEstimate(
            flops=8 * slots * tokens * width * width,
            bytes_accessed=2 * weights.size + 6 * half * tokens * width,
            transcendentals=0,
        ),
    )(source, target, panel, weights)


def fetch(parts, hidden, sems):
    copies = []
    start = 0
    for number, part in enumerate(parts):
        count = part.shape[0]
        copies.append(pltpu.make_async_copy(part, hidden.at[pl.ds(start, count)], sems.at[number]))
        copies[-1].start()
        start += count
    for copy in copies:
        copy.wait()


def to_model_kernel(transposed, pieces, with_sums, with_grads, carried, model_at, hidden_at, live, *refs):
    refs = list(refs)
    panel = refs.pop(0) if with_grads else None
    weights = refs.pop(0) if with_sums else None
    hidden_parts = [refs.pop(0) for _ in range(pieces)]
    carried_in = refs.pop(0) if carried else None
    grads = refs.pop(0) if with_grads else None
    own, send = [refs.pop(0) for _ in range(2)] if with_sums else (None, None)
    carried_out = refs.pop(0) if carried else None
    totals = refs.pop(0) if with_sums else None
    hidden, sems = refs
    step = pl.program_id(0)
    width = hidden.shape[-1]

    @pl.when(step == 0)
    def _():
        if with_sums:
            totals[...] = jnp.zeros(totals.shape, jnp.float32)
        fetch(hidden_parts, hidden, sems)

    if carried:
        carried_out[...] = carried_in[...]

    for slot in range(CHUNK):
        k = step * CHUNK + slot
        model = model_at[k]
        values = hidden[hidden_at[k]]
        is_live = live[k] > 0
        if with_sums:
            term = contract(values, weights[slot], 1, 1 if transposed else 0)
            totals[jnp.where(is_live, model, totals.shape[0] - 1)] += term
        if with_grads:
            other = lanes(panel, model, width)
            if transposed:
                grad = contract(other, values, 0, 0)
            else:
                grad = contract(values, other, 0, 0)
            grads[slot] = jnp.where(is_live, grad, 0.0).astype(jnp.bfloat16)

    if with_sums:

        @pl.when(step == pl.num_programs(0) - 1)
        def _():
            share = own.shape[0]
            for segment in range(totals.shape[0] - 1):
                columns = pl.ds(segment * width, width)
                own[:, columns] = totals[segment, pl.ds(0, share), :]
                for number, piece in enumerate(send):
                    rows = pl.ds((number + 1) * share, share)
                    piece[:, columns] = totals[segment, rows, :].astype(jnp.bfloat16)


def to_model(
    panel,
    hidden_parts,
    weights,
    places,
    members,
    transposed,
    with_sums=True,
    with_grads=True,
    carried=None,
):
    tokens, columns = panel.shape
    slots, width, _ = weights.shape
    segments = columns // width
    share = tokens // members
    hidden_count = sum(part.shape[0] for part in hidden_parts)
    pieces = len(hidden_parts)
    chunk_spec = pl.BlockSpec((CHUNK, width, width), lambda s, a, b, c: (s, 0, 0))
    share_spec = pl.BlockSpec((share, columns), lambda s, a, b, c: (0, 0))
    operands, in_specs, out_specs, out_shape, scratch = [], [], [], [], []
    if with_grads:
        operands.append(panel)
        in_specs.append(pl.BlockSpec(panel.shape, lambda s, a, b, c: (0, 0)))
        out_specs.append(chunk_spec)
        out_shape.append(jax.ShapeDtypeStruct(weights.shape, jnp.bfloat16))
    if with_sums:
        operands.append(weights)
        in_specs.append(chunk_spec)
        out_specs += [share_spec, [share_spec] * (members - 1)]
        out_shape += [
            jax.ShapeDtypeStruct((share, columns), jnp.float32),
            [jax.ShapeDtypeStruct((share, columns), jnp.bfloat16)] * (members - 1),
        ]
        scratch.append(pltpu.VMEM((segments + 1, tokens, width), jnp.float32))
    scratch += [
        pltpu.VMEM((hidden_count, tokens, width), jnp.bfloat16),
        pltpu.SemaphoreType.DMA((pieces,)),
    ]
    extra, extra_specs = [], []
    if carried is not None:
        extra = [carried]
        carried_spec = pl.BlockSpec(
            (CHUNK // 2, 2 * width, width), lambda s, a, b, c: (s, 0, 0)
        )
        extra_specs.append(carried_spec)
        out_specs.append(carried_spec)
        out_shape.append(jax.ShapeDtypeStruct(carried.shape, carried.dtype))

    def kernel(*refs):
        flat = list(refs)
        if with_sums:
            start = 3 + len(operands) + pieces + len(extra) + (1 if with_grads else 0) + 1
            if not isinstance(flat[start], (list, tuple)):
                flat[start : start + members - 1] = [flat[start : start + members - 1]]
        to_model_kernel(transposed, pieces, with_sums, with_grads, carried is not None, *flat)

    return pl.pallas_call(
        kernel,
        grid_spec=pltpu.PrefetchScalarGridSpec(
            num_scalar_prefetch=3,
            grid=(slots // CHUNK,),
            in_specs=in_specs + [pl.BlockSpec(memory_space=pl.ANY)] * pieces + extra_specs,
            out_specs=out_specs,
            scratch_shapes=scratch,
        ),
        out_shape=out_shape,
        compiler_params=pltpu.CompilerParams(vmem_limit_bytes=VMEM_LIMIT),
        cost_estimate=pl.CostEstimate(
            flops=8 * slots * tokens * width * width * (with_sums + with_grads),
            bytes_accessed=4 * weights.size + 2 * hidden_count * tokens * width,
            transcendentals=0,
        ),
    )(*places, *operands, *hidden_parts, *extra)


def swap(values, bit):
    count = lax.axis_size("row")
    return lax.ppermute(values, "row", [(s, s ^ (1 << bit)) for s in range(count)])


def swap_orders():
    rest = list(range(1, int(math.log2(lax.axis_size("row")))))
    return [rest, rest[::-1]]


def hidden_position(index, segments):
    level = int(math.log2(segments))
    row = lax.axis_index("row")
    masks = []
    for order in swap_orders():
        mask = (row & 1) << (level - 1)
        for number, bit in enumerate(order):
            mask = mask | (((row >> bit) & 1) << (level - 3 - number))
        masks.append(mask)
    is_late = ((index >> (level - 2)) & 1) > 0
    return index ^ jnp.where(is_late, masks[1], masks[0])


def after(values, *earlier):
    return lax.optimization_barrier((values, earlier))[0]


def added(terms, start, count):
    total = None
    for array, base in terms:
        piece = array[base + start : base + start + count].astype(jnp.float32)
        total = piece if total is None else total + piece
    return total


GELU_SCALE = math.sqrt(2.0 / math.pi)


def gelu_and_slope(values):
    square = values * values
    bent = jnp.tanh(GELU_SCALE * (values + 0.044715 * (values * square)))
    half = 0.5 * (1.0 + bent)
    slope = half + (0.5 * GELU_SCALE) * values * (1.0 - bent * bent) * (
        1.0 + (3.0 * 0.044715) * square
    )
    return values * half, slope


GROUP = 32
AHEAD = 2
EXCHANGE_LIMIT = 62 * 1024 * 1024


def exchange_kernel(sizes, *refs):
    quarter, own, bits, members = sizes
    refs = list(refs)
    source_at, carries, ends, filled = refs[0:4]
    hidden_at, alive, sorted_at, block_at, chain, part_ends, part_filled = refs[4:11]
    pre_keep, pre_send, cotangent, weights = refs[11:15]
    hidden, spread_back, grads, output = refs[15:19]
    (parts, hold, back_all, stage_out, stage_in, own_hidden, own_back) = refs[19:26]
    (panel, tiles, blocks, running, sums, slopes, out, landing, chosen) = refs[26:35]
    local_sems, block_sems, grad_sems, send_sems, recv_sems = refs[35:]
    half = quarter // 2
    row = lax.axis_index("row")
    col = lax.axis_index("col")
    orders = [list(range(1, bits)), list(range(1, bits))[::-1]]
    tokens, width = parts.shape[1:]
    acc = [parts.at[pl.ds(n * half, half)] for n in range(2)]
    back = [back_all.at[n] for n in range(2)]
    core_in = [hold.at[pl.ds(n * quarter, quarter)] for n in range(2)]
    back_in = [hold.at[pl.ds((2 + n) * quarter, quarter)] for n in range(2)]
    share = tokens // members
    slots = weights.shape[0]
    groups = slots // GROUP
    strip = 32
    started = []
    counts = [0, 0]

    def local(source, target):
        copy = pltpu.make_async_copy(source, target, local_sems.at[counts[0]])
        counts[0] += 1
        copy.start()
        return copy

    def remote_to(source, target, device):
        copy = pltpu.make_async_remote_copy(
            src_ref=source,
            dst_ref=target,
            send_sem=send_sems.at[counts[1]],
            recv_sem=recv_sems.at[counts[1]],
            device_id=device,
            device_id_type=pl.DeviceIdType.MESH,
        )
        counts[1] += 1
        copy.start()
        started.append(copy)
        return copy

    def remote(source, target, bit):
        return remote_to(source, target, {"row": row ^ (1 << bit)})

    def over(count, step):
        def each(index, carry):
            for start in range(0, tokens, strip):
                step(index, pl.ds(start, strip))
            return carry

        lax.fori_loop(0, count, each, 0)

    def fetch_group(group):
        place = lax.rem(group, AHEAD)
        return pltpu.make_async_copy(
            weights.at[pl.ds(group * GROUP, GROUP)], blocks.at[place], block_sems.at[place]
        )

    loads = [local(pre_keep.at[pl.ds(n * quarter + half, half)], acc[n]) for n in range(2)]
    own_tokens = local(cotangent, panel.at[pl.ds(0, share)])
    for group in range(min(AHEAD, groups)):
        fetch_group(group).start()

    barrier = pltpu.get_barrier_semaphore()
    for bit in range(bits):
        pl.semaphore_signal(
            barrier,
            inc=1,
            device_id={"row": row ^ (1 << bit)},
            device_id_type=pl.DeviceIdType.MESH,
        )
    for distance in range(1, members):
        pl.semaphore_signal(
            barrier,
            inc=1,
            device_id={"col": lax.rem(col + distance, members)},
            device_id_type=pl.DeviceIdType.MESH,
        )
    pl.semaphore_wait(barrier, bits + members - 1)

    low = half // 2
    spans = ((half + low, low), (half, low), (0, half))

    def swap_core(n, span, source, target):
        return remote(source, target[n].at[pl.ds(*span)], 0)

    pre_core = [[], []]
    for span in spans:
        for n in range(2):
            source = pre_send.at[pl.ds(n * quarter + span[0], span[1])]
            pre_core[n].append(swap_core(n, span, source, core_in))
    arrivals = []
    for distance in range(1, members):
        slot = pl.ds((members - distance) * share, share)
        device = {"col": lax.rem(col + distance, members)}
        arrivals.append(remote_to(cotangent, panel.at[slot], device))

    pre_stages = []
    out_places = [0]
    in_places = [0]

    def stage_send(n, bit, count, value, ready):
        base, there = out_places[0], in_places[0]
        out_places[0] += count
        in_places[0] += count
        cut = count // 2
        copies = []
        for number, (start, size) in enumerate(((cut, count - cut), (0, cut))):
            ready[number]()

            def step(index, rows):
                stage_out[base + start + index, rows] = value(start + index, rows).astype(
                    jnp.bfloat16
                )

            over(size, step)
            copies.append(
                remote(
                    stage_out.at[pl.ds(base + start, size)],
                    stage_in.at[pl.ds(there + start, size)],
                    bit,
                )
            )
        pre_stages.append((copies, there))
        return copies, there

    def nothing():
        return None

    def arrived_at(base):
        return lambda i, r: stage_in[base + i, r].astype(jnp.float32)

    def pass_on(ref, n, flight, count, bit):
        copies, base = flight
        lower = count // 2
        copies[0].wait_recv()
        term = arrived_at(base)
        return stage_send(
            n,
            bit,
            lower,
            lambda i, r: ref[n][lower + i, r] + term(lower + i, r),
            (nothing, nothing),
        )

    def fold(ref, n, count, term):
        def step(i, r):
            ref[n][i, r] = ref[n][i, r] + term(i, r)

        over(count, step)

    def fold_rest(ref, n, flight, count):
        copies, base = flight
        copies[1].wait_recv()
        fold(ref, n, count // 2, arrived_at(base))

    def product(group, carry):
        fetch_group(group).wait()
        place = lax.rem(group, AHEAD)
        total = running[...]
        for slot in range(GROUP):
            k = group * GROUP + slot
            term = contract(tiles[source_at[k]], blocks[place, slot], 1, 1)
            total = total * carries[k] + term
            sums[k] = total.astype(jnp.bfloat16)
        running[...] = total

        @pl.when(group + AHEAD < groups)
        def _():
            fetch_group(group + AHEAD).start()

        return carry

    def summed(position, rows):
        return sums[ends[position], rows].astype(jnp.float32) * filled[position]

    def spread(target, n, stages, source, start, size, at, landed, number):
        for later in range(number, len(stages)):
            place = at + start + (own << later)
            copy = remote(source, target.at[pl.ds(place, size)], stages[later])
            landed[later].append((start + (own << later), size, copy))

    def forward(target, n, stages, at, landed, number):
        for start, size, copy in landed[number]:
            copy.wait_recv()
            piece = target.at[pl.ds(at + start, size)]
            spread(target, n, stages, piece, start, size, at, landed, number + 1)

    def cross(source, target, at, start, size):
        far_copies.append(remote(source, target.at[pl.ds(at + start, size)], 0))

    def move_on(target, landed, number):
        for n in range(2):
            at = n * quarter
            forward(target, n, to_hidden_stages[n], at, landed[n], number)
            for start, size, _ in landed[n][number]:
                piece = target.at[pl.ds(at + start, size)]
                cross(piece, target, 2 * quarter + at, start, size)

    far_copies = []
    to_hidden_stages = [order[::-1] for order in orders]
    hidden_landed = [[[] for _ in stages] for stages in to_hidden_stages]
    back_landed = [[[] for _ in stages] for stages in to_hidden_stages]
    cut = own // 2
    own_spans = ((cut, own - cut), (0, cut))

    pre_flight = [None, None]
    for n in range(2):
        loads[n].wait()
        pre_flight[n] = stage_send(
            n,
            orders[n][0],
            half,
            lambda i, r, n=n: acc[n][i, r] + core_in[n][half + i, r].astype(jnp.float32),
            (pre_core[n][0].wait_recv, pre_core[n][1].wait_recv),
        )
        loads[n] = local(pre_keep.at[pl.ds(n * quarter, half)], acc[n])
    for n in range(2):
        loads[n].wait()
        pre_core[n][2].wait_recv()
        fold(acc, n, half, lambda i, r: core_in[n][i, r].astype(jnp.float32))
    running[...] = jnp.zeros(running.shape, jnp.float32)

    count = half
    marks = [0, groups // 3, 2 * groups // 3, groups]
    for number, _ in enumerate(orders[0][1:]):
        flights = [
            pass_on(acc, n, pre_flight[n], count, orders[n][1 + number]) for n in range(2)
        ]
        if number == 0:
            own_tokens.wait()
            for copy in arrivals:
                copy.wait_recv()
            for tile in range(tiles.shape[0]):
                tiles[tile] = panel[:, tile * width : (tile + 1) * width]
            lax.fori_loop(marks[0], marks[1], product, 0)
        for n in range(2):
            fold_rest(acc, n, pre_flight[n], count)
        pre_flight = flights
        count = count // 2
    lax.fori_loop(marks[1], marks[2], product, 0)

    kept = []
    for number, (start, size) in enumerate(own_spans):
        for n in range(2):
            copies, base = pre_flight[n]
            copies[number].wait_recv()

            def act(index, r):
                i = start + index
                value, slope = gelu_and_slope(
                    acc[n][i, r] + stage_in[base + i, r].astype(jnp.float32)
                )
                own_hidden[n, i, r] = value.astype(jnp.bfloat16)
                slopes[n, i, r] = slope

            over(size, act)
            piece = own_hidden.at[n, pl.ds(start, size)]
            at = n * quarter
            spread(
                hidden, n, to_hidden_stages[n], piece, start, size, at, hidden_landed[n], 0
            )
            cross(piece, hidden, 2 * quarter + at, start, size)
            kept.append(local(piece, hidden.at[pl.ds(at + start, size)]))
        if number == 0:
            lax.fori_loop(marks[2], marks[3], product, 0)

    for copies, _ in pre_stages:
        for copy in copies:
            copy.wait_send()
            started[:] = [other for other in started if other is not copy]
    out_places[0] = 0
    back_core = [[], []]
    for first, size in spans:
        for n in range(2):

            def step(i, r):
                value = summed(2 * quarter + n * quarter + first + i, r)
                core_in[n][first + i, r] = value.astype(jnp.bfloat16)

            over(size, step)
            source = core_in[n].at[pl.ds(first, size)]
            back_core[n].append(swap_core(n, (first, size), source, back_in))
    back_flight = [None, None]
    move_on(hidden, hidden_landed, 0)
    for n in range(2):
        back_flight[n] = stage_send(
            n,
            orders[n][0],
            half,
            lambda i, r, n=n: summed(n * quarter + half + i, r)
            + back_in[n][half + i, r].astype(jnp.float32),
            (back_core[n][0].wait_recv, back_core[n][1].wait_recv),
        )
    for n in range(2):
        back_core[n][2].wait_recv()

        def begin(i, r):
            back[n][i, r] = summed(n * quarter + i, r) + back_in[n][i, r].astype(jnp.float32)

        over(half, begin)
    for copies in back_core:
        for copy in copies:
            copy.wait_send()
            started[:] = [other for other in started if other is not copy]

    for number in range(1, len(to_hidden_stages[0])):
        move_on(hidden, hidden_landed, number)
    for copy in kept:
        copy.wait()
    kept.clear()
    for copy in far_copies:
        copy.wait_recv()
    far_copies.clear()
    filled_in = [
        local(hidden.at[pl.ds(n * quarter, quarter)], hold.at[pl.ds(n * quarter, quarter)])
        for n in range(4)
    ]

    out[...] = jnp.zeros(out.shape, jnp.float32)
    pairs = GROUP // 2

    def grad_copy(group):
        here = pl.ds(group * pairs, pairs)
        return pltpu.make_async_copy(sums.at[here], grads.at[here], grad_sems.at[group])

    def forward_product(group, carry):
        fetch_group(group).wait()
        place = lax.rem(group, AHEAD)
        for slot in range(GROUP):
            k = group * GROUP + slot
            grad = contract(hold[hidden_at[k]], tiles[source_at[k]], 0, 0) * alive[k]
            rows = pl.ds(slot % 2 * width, width)
            sums[group * pairs + slot // 2, rows] = grad.astype(jnp.bfloat16)
        grad_copy(group).start()
        for slot in range(GROUP):
            chosen[slot] = blocks[place, slot]
        total = None
        for slot in range(GROUP):
            source = hold[sorted_at[group, slot]]
            term = contract(source, chosen[block_at[group, slot]], 1, 0)
            total = term if slot == 0 else total * chain[group, slot] + term
            parts[slot] = total

        def flush(tile, inner):
            end, factor = part_ends[group, tile], part_filled[group, tile]
            for start in range(0, tokens, strip):
                rows = pl.ds(start, strip)
                out[tile, rows] = out[tile, rows] + parts[end, rows] * factor
            return inner

        lax.fori_loop(0, out.shape[0], flush, 0)

        @pl.when(group + AHEAD < groups)
        def _():
            fetch_group(group + AHEAD).start()

        return carry

    for group in range(min(AHEAD, groups)):
        fetch_group(group).start()
    for copy in filled_in:
        copy.wait()
    steps = [0, groups // 6, groups // 2, 2 * groups // 3, 3 * groups // 4, groups]
    lax.fori_loop(steps[0], steps[1], forward_product, 0)

    count = half
    for number, _ in enumerate(orders[0][1:]):
        flights = [
            pass_on(back, n, back_flight[n], count, orders[n][1 + number]) for n in range(2)
        ]
        if number == 0:
            lax.fori_loop(steps[1], steps[2], forward_product, 0)
        for n in range(2):
            fold_rest(back, n, back_flight[n], count)
        back_flight = flights
        count = count // 2
    lax.fori_loop(steps[2], steps[3], forward_product, 0)

    for number, (start, size) in enumerate(own_spans):
        for n in range(2):
            copies, base = back_flight[n]
            copies[number].wait_recv()

            def slope_times(index, r):
                i = start + index
                value = back[n][i, r] + stage_in[base + i, r].astype(jnp.float32)
                own_back[n, i, r] = (value * slopes[n, i, r]).astype(jnp.bfloat16)

            over(size, slope_times)
            piece = own_back.at[n, pl.ds(start, size)]
            at = n * quarter
            spread(
                spread_back, n, to_hidden_stages[n], piece, start, size, at, back_landed[n], 0
            )
            cross(piece, spread_back, 2 * quarter + at, start, size)
            kept.append(local(piece, spread_back.at[pl.ds(at + start, size)]))
        if number == 0:
            lax.fori_loop(steps[3], steps[4], forward_product, 0)
    lax.fori_loop(steps[4], steps[5], forward_product, 0)

    for tile in range(out.shape[0]):
        panel[:, tile * width : (tile + 1) * width] = out[tile].astype(jnp.bfloat16)
    shares = []
    for distance in range(1, members):
        device = {"col": lax.rem(col + distance, members)}
        source = panel.at[pl.ds(distance * share, share)]
        slot = pl.ds((distance - 1) * share, share)
        shares.append(remote_to(source, landing.at[slot], device))
    for number in range(len(to_hidden_stages[0])):
        move_on(spread_back, back_landed, number)
    for copy in shares:
        copy.wait_recv()
    for tile in range(out.shape[0]):
        columns = slice(tile * width, (tile + 1) * width)
        total = out[tile, 0:share]
        for number in range(members - 1):
            rows = slice(number * share, (number + 1) * share)
            total = total + landing[rows, columns].astype(jnp.float32)
        output[:, columns] = total
    for copy in kept:
        copy.wait()
    for copy in far_copies:
        copy.wait_recv()

    def grads_done(group, carry):
        grad_copy(group).wait()
        return carry

    lax.fori_loop(0, groups, grads_done, 0)
    for copy in started:
        copy.wait_send()


def exchange(pre_keep, pre_send, cotangent, weights, scalars):
    held, tokens, width = pre_keep.shape
    share, columns = cotangent.shape
    slots = weights.shape[0]
    segments = 2 * held
    quarter = held // 2
    half = quarter // 2
    bits = int(math.log2(lax.axis_size("row")))
    members = lax.axis_size("col")
    own = quarter >> (bits - 1)
    staged = 2 * (quarter - own)
    copies = 2 * (members - 1) + 12 + 8 * (bits - 1) + 16 * (quarter // own)
    wide, narrow = jnp.float32, jnp.bfloat16
    pair_shape = (slots // 2, 2 * width, width)
    tiles = columns // width
    out_shape = [jax.ShapeDtypeStruct((segments, tokens, width), narrow)] * 2
    out_shape += [
        jax.ShapeDtypeStruct(pair_shape, narrow),
        jax.ShapeDtypeStruct((share, columns), wide),
    ]
    return pl.pallas_call(
        functools.partial(exchange_kernel, (quarter, own, bits, members)),
        in_specs=[pl.BlockSpec(memory_space=pltpu.SMEM)] * len(scalars)
        + [pl.BlockSpec(memory_space=pl.ANY)] * 4,
        out_specs=[pl.BlockSpec(memory_space=pl.ANY)] * 3
        + [pl.BlockSpec(memory_space=pltpu.VMEM)],
        out_shape=out_shape,
        scratch_shapes=[
            pltpu.VMEM((max(2 * half, GROUP), tokens, width), wide),
            pltpu.VMEM((4 * quarter, tokens, width), narrow),
            pltpu.VMEM((2, half, tokens, width), wide),
            pltpu.VMEM((staged, tokens, width), narrow),
            pltpu.VMEM((2 * staged, tokens, width), narrow),
            pltpu.VMEM((2, own, tokens, width), narrow),
            pltpu.VMEM((2, own, tokens, width), narrow),
            pltpu.VMEM((tokens, columns), narrow),
            pltpu.VMEM((tiles, tokens, width), narrow),
            pltpu.VMEM((AHEAD, GROUP, width, width), narrow),
            pltpu.VMEM((tokens, width), wide),
            pltpu.VMEM((slots, tokens, width), narrow),
            pltpu.VMEM((2, own, tokens, width), wide),
            pltpu.VMEM((tiles, tokens, width), wide),
            pltpu.VMEM((tokens - share, columns), narrow),
            pltpu.VMEM((GROUP, width, width), narrow),
            pltpu.SemaphoreType.DMA((24,)),
            pltpu.SemaphoreType.DMA((AHEAD,)),
            pltpu.SemaphoreType.DMA((slots // GROUP,)),
            pltpu.SemaphoreType.DMA((copies,)),
            pltpu.SemaphoreType.DMA((copies,)),
        ],
        compiler_params=pltpu.CompilerParams(
            collective_id=1, has_side_effects=True, vmem_limit_bytes=EXCHANGE_LIMIT
        ),
        cost_estimate=pl.CostEstimate(
            flops=24 * slots * tokens * width * width,
            bytes_accessed=30 * segments * tokens * width // 2,
            transcendentals=2 * own * tokens * width,
        ),
    )(*scalars, pre_keep, pre_send, cotangent, weights)


def group_order(model, hidden, live, tiles):
    slots = model.shape[0]
    key = jnp.where(live > 0, model, tiles).reshape(-1, GROUP)
    place = jnp.arange(GROUP, dtype=jnp.int32)
    first = (key[:, None, :] < key[:, :, None]) | (
        (key[:, None, :] == key[:, :, None]) & (place[None, :] < place[:, None])
    )
    rank = jnp.sum(first.astype(jnp.int32), axis=2)
    chosen = rank[:, None, :] == place[None, :, None]

    def pick(values):
        return jnp.sum(jnp.where(chosen, values[:, None, :], 0), axis=2)

    spot = jnp.broadcast_to(place[None, :], key.shape)
    ordered = pick(key)
    chain = jnp.concatenate(
        [jnp.zeros_like(ordered[:, :1]), (ordered[:, 1:] == ordered[:, :-1]).astype(jnp.int32)],
        axis=1,
    ).astype(jnp.float32)
    targets = jnp.arange(tiles, dtype=jnp.int32)
    lasts = jnp.max(
        jnp.where(ordered[:, None, :] == targets[None, :, None], spot[:, None, :], -1), axis=2
    )
    ordered_fields = [pick(hidden.reshape(-1, GROUP)), pick(spot), chain, jnp.maximum(lasts, 0)]
    ordered_fields.append((lasts >= 0).astype(jnp.float32))
    return ordered_fields


RELAY_ROWS = 16


def relay_kernel(members, own_ref, all_ref, local_sem, send_sems, recv_sems):
    share = own_ref.shape[0]
    pieces = share // RELAY_ROWS
    me = lax.axis_index("col")
    hops = members - 1

    def place(block, device, piece):
        slot = (block - device + members) % members
        return pl.ds(pl.multiple_of(slot * share + piece * RELAY_ROWS, RELAY_ROWS), RELAY_ROWS)

    mine = pltpu.make_async_copy(own_ref, all_ref.at[pl.ds(0, share)], local_sem)
    mine.start()
    barrier = pltpu.get_barrier_semaphore()
    for step in (1, -1):
        inside = (me + step >= 0) & (me + step < members)

        @pl.when(inside)
        def _():
            pl.semaphore_signal(
                barrier,
                inc=1,
                device_id={"col": me + step},
                device_id_type=pl.DeviceIdType.MESH,
            )

    pl.semaphore_wait(barrier, jnp.where((me > 0) & (me < members - 1), 2, 1))

    def move(side, hop, piece):
        step = 1 if side == 0 else -1
        block = me - step * hop
        target = jnp.clip(me + step, 0, members - 1)
        block = jnp.clip(block, 0, members - 1)
        if hop == 0:
            source = own_ref.at[pl.ds(piece * RELAY_ROWS, RELAY_ROWS)]
        else:
            source = all_ref.at[place(block, me, piece)]
        at = (side * hops + hop) * pieces + piece
        return pltpu.make_async_remote_copy(
            src_ref=source,
            dst_ref=all_ref.at[place(block, target, piece)],
            send_sem=send_sems.at[at],
            recv_sem=recv_sems.at[at],
            device_id={"col": target},
            device_id_type=pl.DeviceIdType.MESH,
        )

    def exists(side, hop):
        step = 1 if side == 0 else -1
        block = me - step * hop
        target = me + step
        return (block >= 0) & (block < members) & (target >= 0) & (target < members)

    def comes(side, hop):
        step = 1 if side == 0 else -1
        block = me - step * (hop + 1)
        return (block >= 0) & (block < members)

    for hop in range(members):
        for piece in range(pieces):
            for side in range(2):
                if hop > 0:

                    @pl.when(comes(side, hop - 1))
                    def _():
                        move(side, hop - 1, piece).wait_recv()

                if hop < hops:

                    @pl.when(exists(side, hop))
                    def _():
                        move(side, hop, piece).start()

    for hop in range(hops):
        for piece in range(pieces):
            for side in range(2):

                @pl.when(exists(side, hop))
                def _():
                    move(side, hop, piece).wait_send()

    mine.wait()


def relay_tokens(values):
    members = lax.axis_size("col")
    share, columns = values.shape
    copies = 2 * (members - 1) * (share // RELAY_ROWS)
    return pl.pallas_call(
        functools.partial(relay_kernel, members),
        in_specs=[pl.BlockSpec(memory_space=pl.ANY)],
        out_specs=pl.BlockSpec(memory_space=pl.ANY),
        out_shape=jax.ShapeDtypeStruct((members * share, columns), values.dtype),
        scratch_shapes=[
            pltpu.SemaphoreType.DMA,
            pltpu.SemaphoreType.DMA((copies,)),
            pltpu.SemaphoreType.DMA((copies,)),
        ],
        compiler_params=pltpu.CompilerParams(collective_id=2, has_side_effects=True),
    )(values)


def shift(values, distance):
    count = lax.axis_size("col")
    return lax.ppermute(values, "col", [(s, (s + distance) % count) for s in range(count)])


def gather_tokens(values):
    count = lax.axis_size("col")
    return jnp.concatenate([values] + [shift(values, -d) for d in range(1, count)], axis=0)


def scatter_tokens(own, send):
    total = own
    for number, piece in enumerate(send):
        total = total + shift(piece, number + 1).astype(jnp.float32)
    return total


def body(activations, grad_out, first_blocks, first_coords, second_blocks, second_coords):
    width = first_blocks.shape[-1]
    members = lax.axis_size("col")
    row_tiles = activations.shape[1] // width
    col_tiles = FF // width // members
    row_base = lax.axis_index("row") * row_tiles
    col_base = lax.axis_index("col") * col_tiles

    def fields(model, hidden):
        is_live = model >= 0
        model_at = jnp.where(is_live, model - row_base, 0)
        hidden_at = jnp.where(is_live, hidden_position(hidden - col_base, col_tiles), 0)
        target = jnp.where(is_live, hidden_at, col_tiles)
        return model_at, hidden_at, target, is_live.astype(jnp.int32)

    model_one, hidden_one, target_one, live_one = fields(
        first_coords[0, 0, :, 0], first_coords[0, 0, :, 1]
    )
    model_two, hidden_two, target_two, live_two = fields(
        second_coords[0, 0, :, 1], second_coords[0, 0, :, 0]
    )
    weights_one = first_blocks[0, 0]
    weights_two = second_blocks[0, 0]

    inputs_all = relay_tokens(activations)
    pre_keep, pre_send = to_hidden(
        inputs_all, weights_one, model_one, target_one, col_tiles, False
    )
    same = (target_two[1:] == target_two[:-1]).astype(jnp.float32)
    carries = jnp.concatenate([jnp.zeros((1,), jnp.float32), same])
    numbers = jnp.arange(target_two.shape[0], dtype=jnp.int32)
    places = jnp.arange(col_tiles, dtype=jnp.int32)
    lasts = jnp.max(
        jnp.where(target_two[None, :] == places[:, None], numbers[None, :], -1), axis=1
    )
    ends = jnp.maximum(lasts, 0)
    filled = (lasts >= 0).astype(jnp.float32)
    alive_two = live_two.astype(jnp.float32)
    scalars = [model_two, carries, ends, filled, hidden_two, alive_two]
    scalars += group_order(model_two, hidden_two, live_two, grad_out.shape[1] // width)
    _, grad_pre, grads_two, output = exchange(
        pre_keep, pre_send, grad_out, weights_two, scalars
    )
    grad_pre_parts = [grad_pre]
    places_one = (model_one, hidden_one, live_one)
    own_in, send_in, grad_second = to_model(
        inputs_all,
        grad_pre_parts,
        weights_one,
        places_one,
        members,
        True,
        with_grads=False,
        carried=grads_two,
    )
    grad_second = grad_second.reshape(second_blocks.shape[2:])
    grad_input = scatter_tokens(own_in, send_in)
    (grad_first,) = to_model(
        inputs_all,
        after(grad_pre_parts, own_in, output),
        weights_one,
        places_one,
        members,
        True,
        with_sums=False,
    )
    return (output, grad_input, grad_first[None, None], grad_second[None, None])


def solution(mesh):
    return jax.shard_map(
        body,
        mesh=mesh,
        in_specs=(
            P("col", "row"),
            P("col", "row"),
            P("row", "col", None, None, None),
            P("row", "col", None, None),
            P("col", "row", None, None, None),
            P("col", "row", None, None),
        ),
        out_specs=(
            P("col", "row"),
            P("col", "row"),
            P("row", "col", None, None, None),
            P("col", "row", None, None, None),
        ),
        check_vma=False,
    )
```

```python
import functools
import math

import jax
import jax.numpy as jnp
from jax import lax
from jax.experimental import pallas as pl
from jax.experimental.pallas import tpu as pltpu
from jax.sharding import PartitionSpec as P

FF = 65536
CHUNK = 64
VMEM_LIMIT = 58 * 1024 * 1024


def gelu_tanh(values):
    return jax.nn.gelu(values, approximate=True)


def contract(left, right, left_dim, right_dim):
    return lax.dot_general(
        left, right, (((left_dim,), (right_dim,)), ((), ())), preferred_element_type=jnp.float32
    )


def lanes(ref, index, width):
    return ref[:, pl.ds(pl.multiple_of(index * width, width), width)]


OUT_PIECES = 4


def longest_run(slots):
    return next(run for run in (48, 40, 32, 16, 8, 4, 2, 1) if slots % run == 0)


def to_hidden_kernel(source, target, panel, weights, keep, send, totals, blocks, rounded, *sems):
    block_sems, keep_sems, send_sems = sems
    slots, width, _ = weights.shape
    segments = totals.shape[0] - 1
    half = segments // 2
    run = longest_run(slots)
    piece = half // OUT_PIECES

    def load(number):
        here = pl.ds(number * run, run)
        return pltpu.make_async_copy(weights.at[here], blocks.at[here], block_sems.at[number])

    def store(values, number, base, out, out_sems):
        return pltpu.make_async_copy(
            values.at[pl.ds(base + number * piece, piece)],
            out.at[pl.ds(number * piece, piece)],
            out_sems.at[number],
        )

    for number in range(slots // run):
        load(number).start()

    def clear(index, carry):
        totals[index] = jnp.zeros(totals.shape[1:], jnp.float32)
        return carry

    lax.fori_loop(0, segments, clear, 0)

    def add(number, carry):
        load(number).wait()
        for slot in range(run):
            k = number * run + slot
            totals[target[k]] += contract(lanes(panel, source[k], width), blocks[k], 1, 0)
        return carry

    lax.fori_loop(0, slots // run, add, 0)
    for number in range(OUT_PIECES):
        store(totals, number, 0, keep, keep_sems).start()
    for number in range(OUT_PIECES):

        def turn(index, carry):
            at = number * piece + index
            rounded[at] = totals[half + at].astype(jnp.bfloat16)
            return carry

        lax.fori_loop(0, piece, turn, 0)
        store(rounded, number, 0, send, send_sems).start()
    for number in range(OUT_PIECES):
        store(totals, number, 0, keep, keep_sems).wait()
        store(rounded, number, 0, send, send_sems).wait()


def to_hidden(panel, weights, source, target, segments):
    tokens = panel.shape[0]
    slots, width, _ = weights.shape
    half = segments // 2
    return pl.pallas_call(
        to_hidden_kernel,
        grid_spec=pltpu.PrefetchScalarGridSpec(
            num_scalar_prefetch=2,
            grid=(1,),
            in_specs=[
                pl.BlockSpec(panel.shape, lambda s, a, b: (0, 0)),
                pl.BlockSpec(memory_space=pl.ANY),
            ],
            out_specs=[pl.BlockSpec(memory_space=pl.ANY)] * 2,
            scratch_shapes=[
                pltpu.VMEM((segments + 1, tokens, width), jnp.float32),
                pltpu.VMEM((slots, width, width), jnp.bfloat16),
                pltpu.VMEM((half, tokens, width), jnp.bfloat16),
                pltpu.SemaphoreType.DMA((slots // longest_run(slots),)),
                pltpu.SemaphoreType.DMA((OUT_PIECES,)),
                pltpu.SemaphoreType.DMA((OUT_PIECES,)),
            ],
        ),
        out_shape=[
            jax.ShapeDtypeStruct((half, tokens, width), jnp.float32),
            jax.ShapeDtypeStruct((half, tokens, width), jnp.bfloat16),
        ],
        compiler_params=pltpu.CompilerParams(vmem_limit_bytes=VMEM_LIMIT),
        cost_estimate=pl.CostEstimate(
            flops=8 * slots * tokens * width * width,
            bytes_accessed=2 * weights.size + 6 * half * tokens * width,
            transcendentals=0,
        ),
    )(source, target, panel, weights)


def fetch(parts, hidden, sems):
    copies = []
    start = 0
    for number, part in enumerate(parts):
        count = part.shape[0]
        copies.append(pltpu.make_async_copy(part, hidden.at[pl.ds(start, count)], sems.at[number]))
        copies[-1].start()
        start += count
    for copy in copies:
        copy.wait()


def to_model_kernel(transposed, pieces, with_sums, with_grads, carried, chunk, model_at, hidden_at, live, *refs):
    refs = list(refs)
    panel = refs.pop(0) if with_grads else None
    weights = refs.pop(0) if with_sums else None
    hidden_parts = [refs.pop(0) for _ in range(pieces)]
    carried_in = refs.pop(0) if carried else None
    grads = refs.pop(0) if with_grads else None
    own, send = [refs.pop(0) for _ in range(2)] if with_sums else (None, None)
    carried_out = refs.pop(0) if carried else None
    totals = refs.pop(0) if with_sums else None
    hidden, sems = refs
    step = pl.program_id(0)
    width = hidden.shape[-1]

    @pl.when(step == 0)
    def _():
        if with_sums:
            totals[...] = jnp.zeros(totals.shape, jnp.float32)
        fetch(hidden_parts, hidden, sems)

    if carried:
        carried_out[...] = carried_in[...]

    for slot in range(chunk):
        k = step * chunk + slot
        model = model_at[k]
        values = hidden[hidden_at[k]]
        is_live = live[k] > 0
        if with_sums:
            term = contract(values, weights[slot], 1, 1 if transposed else 0)
            totals[jnp.where(is_live, model, totals.shape[0] - 1)] += term
        if with_grads:
            other = lanes(panel, model, width)
            if transposed:
                grad = contract(other, values, 0, 0)
            else:
                grad = contract(values, other, 0, 0)
            grads[slot] = jnp.where(is_live, grad, 0.0).astype(jnp.bfloat16)

    if with_sums:

        @pl.when(step == pl.num_programs(0) - 1)
        def _():
            share = own.shape[0]
            for segment in range(totals.shape[0] - 1):
                columns = pl.ds(segment * width, width)
                own[:, columns] = totals[segment, pl.ds(0, share), :]
                for number, piece in enumerate(send):
                    rows = pl.ds((number + 1) * share, share)
                    piece[:, columns] = totals[segment, rows, :].astype(jnp.bfloat16)


def to_model(
    panel,
    hidden_parts,
    weights,
    places,
    members,
    transposed,
    with_sums=True,
    with_grads=True,
    carried=None,
):
    tokens, columns = panel.shape
    slots, width, _ = weights.shape
    segments = columns // width
    share = tokens // members
    chunk = next(count for count in (CHUNK, CHUNK // 2, 1) if slots % count == 0)
    hidden_count = sum(part.shape[0] for part in hidden_parts)
    pieces = len(hidden_parts)
    chunk_spec = pl.BlockSpec((chunk, width, width), lambda s, a, b, c: (s, 0, 0))
    share_spec = pl.BlockSpec((share, columns), lambda s, a, b, c: (0, 0))
    operands, in_specs, out_specs, out_shape, scratch = [], [], [], [], []
    if with_grads:
        operands.append(panel)
        in_specs.append(pl.BlockSpec(panel.shape, lambda s, a, b, c: (0, 0)))
        out_specs.append(chunk_spec)
        out_shape.append(jax.ShapeDtypeStruct(weights.shape, jnp.bfloat16))
    if with_sums:
        operands.append(weights)
        in_specs.append(chunk_spec)
        out_specs += [share_spec, [share_spec] * (members - 1)]
        out_shape += [
            jax.ShapeDtypeStruct((share, columns), jnp.float32),
            [jax.ShapeDtypeStruct((share, columns), jnp.bfloat16)] * (members - 1),
        ]
        scratch.append(pltpu.VMEM((segments + 1, tokens, width), jnp.float32))
    scratch += [
        pltpu.VMEM((hidden_count, tokens, width), jnp.bfloat16),
        pltpu.SemaphoreType.DMA((pieces,)),
    ]
    extra, extra_specs = [], []
    if carried is not None:
        extra = [carried]
        carried_spec = pl.BlockSpec(
            (chunk // 2, 2 * width, width), lambda s, a, b, c: (s, 0, 0)
        )
        extra_specs.append(carried_spec)
        out_specs.append(carried_spec)
        out_shape.append(jax.ShapeDtypeStruct(carried.shape, carried.dtype))

    def kernel(*refs):
        flat = list(refs)
        if with_sums:
            start = 3 + len(operands) + pieces + len(extra) + (1 if with_grads else 0) + 1
            if not isinstance(flat[start], (list, tuple)):
                flat[start : start + members - 1] = [flat[start : start + members - 1]]
        to_model_kernel(transposed, pieces, with_sums, with_grads, carried is not None, chunk, *flat)

    return pl.pallas_call(
        kernel,
        grid_spec=pltpu.PrefetchScalarGridSpec(
            num_scalar_prefetch=3,
            grid=(slots // chunk,),
            in_specs=in_specs + [pl.BlockSpec(memory_space=pl.ANY)] * pieces + extra_specs,
            out_specs=out_specs,
            scratch_shapes=scratch,
        ),
        out_shape=out_shape,
        compiler_params=pltpu.CompilerParams(vmem_limit_bytes=VMEM_LIMIT),
        cost_estimate=pl.CostEstimate(
            flops=8 * slots * tokens * width * width * (with_sums + with_grads),
            bytes_accessed=4 * weights.size + 2 * hidden_count * tokens * width,
            transcendentals=0,
        ),
    )(*places, *operands, *hidden_parts, *extra)


def swap(values, bit):
    count = lax.axis_size("row")
    return lax.ppermute(values, "row", [(s, s ^ (1 << bit)) for s in range(count)])


def swap_orders():
    rest = list(range(1, int(math.log2(lax.axis_size("row")))))
    return [rest, rest[::-1]]


def hidden_position(index, segments):
    level = int(math.log2(segments))
    row = lax.axis_index("row")
    masks = []
    for order in swap_orders():
        mask = (row & 1) << (level - 1)
        for number, bit in enumerate(order):
            mask = mask | (((row >> bit) & 1) << (level - 3 - number))
        masks.append(mask)
    is_late = ((index >> (level - 2)) & 1) > 0
    return index ^ jnp.where(is_late, masks[1], masks[0])


def after(values, *earlier):
    return lax.optimization_barrier((values, earlier))[0]


def added(terms, start, count):
    total = None
    for array, base in terms:
        piece = array[base + start : base + start + count].astype(jnp.float32)
        total = piece if total is None else total + piece
    return total


GELU_SCALE = math.sqrt(2.0 / math.pi)


def gelu_and_slope(values):
    square = values * values
    bent = jnp.tanh(GELU_SCALE * (values + 0.044715 * (values * square)))
    half = 0.5 * (1.0 + bent)
    slope = half + (0.5 * GELU_SCALE) * values * (1.0 - bent * bent) * (
        1.0 + (3.0 * 0.044715) * square
    )
    return values * half, slope


GROUP = 32
AHEAD = 2
EXCHANGE_LIMIT = 62 * 1024 * 1024


def exchange_kernel(sizes, *refs):
    quarter, own, bits, members = sizes
    refs = list(refs)
    source_at, carries, ends, filled = refs[0:4]
    hidden_at, alive, sorted_at, block_at, chain, part_ends, part_filled = refs[4:11]
    pre_keep, pre_send, cotangent, weights = refs[11:15]
    hidden, spread_back, grads, output = refs[15:19]
    (parts, hold, back_all, stage_out, stage_in, own_hidden, own_back) = refs[19:26]
    (panel, tiles, blocks, running, sums, slopes, out, landing, chosen) = refs[26:35]
    local_sems, block_sems, grad_sems, send_sems, recv_sems = refs[35:]
    half = quarter // 2
    row = lax.axis_index("row")
    col = lax.axis_index("col")
    orders = [list(range(1, bits)), list(range(1, bits))[::-1]]
    tokens, width = parts.shape[1:]
    acc = [parts.at[pl.ds(n * half, half)] for n in range(2)]
    back = [back_all.at[n] for n in range(2)]
    core_in = [hold.at[pl.ds(n * quarter, quarter)] for n in range(2)]
    back_in = [hold.at[pl.ds((2 + n) * quarter, quarter)] for n in range(2)]
    share = tokens // members
    slots = weights.shape[0]
    groups = slots // GROUP
    strip = 32
    started = []
    counts = [0, 0]

    def local(source, target):
        copy = pltpu.make_async_copy(source, target, local_sems.at[counts[0]])
        counts[0] += 1
        copy.start()
        return copy

    def remote_to(source, target, device):
        copy = pltpu.make_async_remote_copy(
            src_ref=source,
            dst_ref=target,
            send_sem=send_sems.at[counts[1]],
            recv_sem=recv_sems.at[counts[1]],
            device_id=device,
            device_id_type=pl.DeviceIdType.MESH,
        )
        counts[1] += 1
        copy.start()
        started.append(copy)
        return copy

    def remote(source, target, bit):
        return remote_to(source, target, {"row": row ^ (1 << bit)})

    def over(count, step):
        def each(index, carry):
            for start in range(0, tokens, strip):
                step(index, pl.ds(start, strip))
            return carry

        lax.fori_loop(0, count, each, 0)

    def fetch_group(group):
        place = lax.rem(group, AHEAD)
        return pltpu.make_async_copy(
            weights.at[pl.ds(group * GROUP, GROUP)], blocks.at[place], block_sems.at[place]
        )

    loads = [local(pre_keep.at[pl.ds(n * quarter + half, half)], acc[n]) for n in range(2)]
    own_tokens = local(cotangent, panel.at[pl.ds(0, share)])
    for group in range(min(AHEAD, groups)):
        fetch_group(group).start()

    barrier = pltpu.get_barrier_semaphore()
    for bit in range(bits):
        pl.semaphore_signal(
            barrier,
            inc=1,
            device_id={"row": row ^ (1 << bit)},
            device_id_type=pl.DeviceIdType.MESH,
        )
    for distance in range(1, members):
        pl.semaphore_signal(
            barrier,
            inc=1,
            device_id={"col": lax.rem(col + distance, members)},
            device_id_type=pl.DeviceIdType.MESH,
        )
    pl.semaphore_wait(barrier, bits + members - 1)

    low = half // 2
    spans = ((half + low, low), (half, low), (0, half))

    def swap_core(n, span, source, target):
        return remote(source, target[n].at[pl.ds(*span)], 0)

    pre_core = [[], []]
    for span in spans:
        for n in range(2):
            source = pre_send.at[pl.ds(n * quarter + span[0], span[1])]
            pre_core[n].append(swap_core(n, span, source, core_in))
    arrivals = []
    for distance in range(1, members):
        slot = pl.ds((members - distance) * share, share)
        device = {"col": lax.rem(col + distance, members)}
        arrivals.append(remote_to(cotangent, panel.at[slot], device))

    pre_stages = []
    out_places = [0]
    in_places = [0]

    def stage_send(n, bit, count, value, ready):
        base, there = out_places[0], in_places[0]
        out_places[0] += count
        in_places[0] += count
        cut = count // 2
        copies = []
        for number, (start, size) in enumerate(((cut, count - cut), (0, cut))):
            ready[number]()

            def step(index, rows):
                stage_out[base + start + index, rows] = value(start + index, rows).astype(
                    jnp.bfloat16
                )

            over(size, step)
            copies.append(
                remote(
                    stage_out.at[pl.ds(base + start, size)],
                    stage_in.at[pl.ds(there + start, size)],
                    bit,
                )
            )
        pre_stages.append((copies, there))
        return copies, there

    def nothing():
        return None

    def arrived_at(base):
        return lambda i, r: stage_in[base + i, r].astype(jnp.float32)

    def pass_on(ref, n, flight, count, bit):
        copies, base = flight
        lower = count // 2
        copies[0].wait_recv()
        term = arrived_at(base)
        return stage_send(
            n,
            bit,
            lower,
            lambda i, r: ref[n][lower + i, r] + term(lower + i, r),
            (nothing, nothing),
        )

    def fold(ref, n, count, term):
        def step(i, r):
            ref[n][i, r] = ref[n][i, r] + term(i, r)

        over(count, step)

    def fold_rest(ref, n, flight, count):
        copies, base = flight
        copies[1].wait_recv()
        fold(ref, n, count // 2, arrived_at(base))

    def product(group, carry):
        fetch_group(group).wait()
        place = lax.rem(group, AHEAD)
        total = running[...]
        for slot in range(GROUP):
            k = group * GROUP + slot
            term = contract(tiles[source_at[k]], blocks[place, slot], 1, 1)
            total = total * carries[k] + term
            sums[k] = total.astype(jnp.bfloat16)
        running[...] = total

        @pl.when(group + AHEAD < groups)
        def _():
            fetch_group(group + AHEAD).start()

        return carry

    def summed(position, rows):
        return sums[ends[position], rows].astype(jnp.float32) * filled[position]

    def spread(target, n, stages, source, start, size, at, landed, number):
        for later in range(number, len(stages)):
            place = at + start + (own << later)
            copy = remote(source, target.at[pl.ds(place, size)], stages[later])
            landed[later].append((start + (own << later), size, copy))

    def forward(target, n, stages, at, landed, number):
        for start, size, copy in landed[number]:
            copy.wait_recv()
            piece = target.at[pl.ds(at + start, size)]
            spread(target, n, stages, piece, start, size, at, landed, number + 1)

    def cross(source, target, at, start, size):
        far_copies.append(remote(source, target.at[pl.ds(at + start, size)], 0))

    def move_on(target, landed, number):
        for n in range(2):
            at = n * quarter
            forward(target, n, to_hidden_stages[n], at, landed[n], number)
            for start, size, _ in landed[n][number]:
                piece = target.at[pl.ds(at + start, size)]
                cross(piece, target, 2 * quarter + at, start, size)

    far_copies = []
    to_hidden_stages = [order[::-1] for order in orders]
    hidden_landed = [[[] for _ in stages] for stages in to_hidden_stages]
    back_landed = [[[] for _ in stages] for stages in to_hidden_stages]
    cut = own // 2
    own_spans = ((cut, own - cut), (0, cut))

    pre_flight = [None, None]
    for n in range(2):
        loads[n].wait()
        pre_flight[n] = stage_send(
            n,
            orders[n][0],
            half,
            lambda i, r, n=n: acc[n][i, r] + core_in[n][half + i, r].astype(jnp.float32),
            (pre_core[n][0].wait_recv, pre_core[n][1].wait_recv),
        )
        loads[n] = local(pre_keep.at[pl.ds(n * quarter, half)], acc[n])
    for n in range(2):
        loads[n].wait()
        pre_core[n][2].wait_recv()
        fold(acc, n, half, lambda i, r: core_in[n][i, r].astype(jnp.float32))
    running[...] = jnp.zeros(running.shape, jnp.float32)

    count = half
    marks = [0, groups // 3, 2 * groups // 3, groups]
    for number, _ in enumerate(orders[0][1:]):
        flights = [
            pass_on(acc, n, pre_flight[n], count, orders[n][1 + number]) for n in range(2)
        ]
        if number == 0:
            own_tokens.wait()
            for copy in arrivals:
                copy.wait_recv()
            for tile in range(tiles.shape[0]):
                tiles[tile] = panel[:, tile * width : (tile + 1) * width]
            lax.fori_loop(marks[0], marks[1], product, 0)
        for n in range(2):
            fold_rest(acc, n, pre_flight[n], count)
        pre_flight = flights
        count = count // 2
    lax.fori_loop(marks[1], marks[2], product, 0)

    kept = []
    for number, (start, size) in enumerate(own_spans):
        for n in range(2):
            copies, base = pre_flight[n]
            copies[number].wait_recv()

            def act(index, r):
                i = start + index
                value, slope = gelu_and_slope(
                    acc[n][i, r] + stage_in[base + i, r].astype(jnp.float32)
                )
                own_hidden[n, i, r] = value.astype(jnp.bfloat16)
                slopes[n, i, r] = slope

            over(size, act)
            piece = own_hidden.at[n, pl.ds(start, size)]
            at = n * quarter
            spread(
                hidden, n, to_hidden_stages[n], piece, start, size, at, hidden_landed[n], 0
            )
            cross(piece, hidden, 2 * quarter + at, start, size)
            kept.append(local(piece, hidden.at[pl.ds(at + start, size)]))
        if number == 0:
            lax.fori_loop(marks[2], marks[3], product, 0)

    for copies, _ in pre_stages:
        for copy in copies:
            copy.wait_send()
            started[:] = [other for other in started if other is not copy]
    out_places[0] = 0
    back_core = [[], []]
    for first, size in spans:
        for n in range(2):

            def step(i, r):
                value = summed(2 * quarter + n * quarter + first + i, r)
                core_in[n][first + i, r] = value.astype(jnp.bfloat16)

            over(size, step)
            source = core_in[n].at[pl.ds(first, size)]
            back_core[n].append(swap_core(n, (first, size), source, back_in))
    back_flight = [None, None]
    move_on(hidden, hidden_landed, 0)
    for n in range(2):
        back_flight[n] = stage_send(
            n,
            orders[n][0],
            half,
            lambda i, r, n=n: summed(n * quarter + half + i, r)
            + back_in[n][half + i, r].astype(jnp.float32),
            (back_core[n][0].wait_recv, back_core[n][1].wait_recv),
        )
    for n in range(2):
        back_core[n][2].wait_recv()

        def begin(i, r):
            back[n][i, r] = summed(n * quarter + i, r) + back_in[n][i, r].astype(jnp.float32)

        over(half, begin)
    for copies in back_core:
        for copy in copies:
            copy.wait_send()
            started[:] = [other for other in started if other is not copy]

    for number in range(1, len(to_hidden_stages[0])):
        move_on(hidden, hidden_landed, number)
    for copy in kept:
        copy.wait()
    kept.clear()
    for copy in far_copies:
        copy.wait_recv()
    far_copies.clear()
    filled_in = [
        local(hidden.at[pl.ds(n * quarter, quarter)], hold.at[pl.ds(n * quarter, quarter)])
        for n in range(4)
    ]

    out[...] = jnp.zeros(out.shape, jnp.float32)
    pairs = GROUP // 2

    def grad_copy(group):
        here = pl.ds(group * pairs, pairs)
        return pltpu.make_async_copy(sums.at[here], grads.at[here], grad_sems.at[group])

    def forward_product(group, carry):
        fetch_group(group).wait()
        place = lax.rem(group, AHEAD)
        for slot in range(GROUP):
            k = group * GROUP + slot
            grad = contract(hold[hidden_at[k]], tiles[source_at[k]], 0, 0) * alive[k]
            rows = pl.ds(slot % 2 * width, width)
            sums[group * pairs + slot // 2, rows] = grad.astype(jnp.bfloat16)
        grad_copy(group).start()
        for slot in range(GROUP):
            chosen[slot] = blocks[place, slot]
        total = None
        for slot in range(GROUP):
            source = hold[sorted_at[group, slot]]
            term = contract(source, chosen[block_at[group, slot]], 1, 0)
            total = term if slot == 0 else total * chain[group, slot] + term
            parts[slot] = total

        def flush(tile, inner):
            end, factor = part_ends[group, tile], part_filled[group, tile]
            for start in range(0, tokens, strip):
                rows = pl.ds(start, strip)
                out[tile, rows] = out[tile, rows] + parts[end, rows] * factor
            return inner

        lax.fori_loop(0, out.shape[0], flush, 0)

        @pl.when(group + AHEAD < groups)
        def _():
            fetch_group(group + AHEAD).start()

        return carry

    for group in range(min(AHEAD, groups)):
        fetch_group(group).start()
    for copy in filled_in:
        copy.wait()
    steps = [0, groups // 6, groups // 2, 2 * groups // 3, 3 * groups // 4, groups]
    lax.fori_loop(steps[0], steps[1], forward_product, 0)

    count = half
    for number, _ in enumerate(orders[0][1:]):
        flights = [
            pass_on(back, n, back_flight[n], count, orders[n][1 + number]) for n in range(2)
        ]
        if number == 0:
            lax.fori_loop(steps[1], steps[2], forward_product, 0)
        for n in range(2):
            fold_rest(back, n, back_flight[n], count)
        back_flight = flights
        count = count // 2
    lax.fori_loop(steps[2], steps[3], forward_product, 0)

    for number, (start, size) in enumerate(own_spans):
        for n in range(2):
            copies, base = back_flight[n]
            copies[number].wait_recv()

            def slope_times(index, r):
                i = start + index
                value = back[n][i, r] + stage_in[base + i, r].astype(jnp.float32)
                own_back[n, i, r] = (value * slopes[n, i, r]).astype(jnp.bfloat16)

            over(size, slope_times)
            piece = own_back.at[n, pl.ds(start, size)]
            at = n * quarter
            spread(
                spread_back, n, to_hidden_stages[n], piece, start, size, at, back_landed[n], 0
            )
            cross(piece, spread_back, 2 * quarter + at, start, size)
            kept.append(local(piece, spread_back.at[pl.ds(at + start, size)]))
        if number == 0:
            lax.fori_loop(steps[3], steps[4], forward_product, 0)
    lax.fori_loop(steps[4], steps[5], forward_product, 0)

    for tile in range(out.shape[0]):
        panel[:, tile * width : (tile + 1) * width] = out[tile].astype(jnp.bfloat16)
    shares = []
    for distance in range(1, members):
        device = {"col": lax.rem(col + distance, members)}
        source = panel.at[pl.ds(distance * share, share)]
        slot = pl.ds((distance - 1) * share, share)
        shares.append(remote_to(source, landing.at[slot], device))
    for number in range(len(to_hidden_stages[0])):
        move_on(spread_back, back_landed, number)
    for copy in shares:
        copy.wait_recv()
    for tile in range(out.shape[0]):
        columns = slice(tile * width, (tile + 1) * width)
        total = out[tile, 0:share]
        for number in range(members - 1):
            rows = slice(number * share, (number + 1) * share)
            total = total + landing[rows, columns].astype(jnp.float32)
        output[:, columns] = total
    for copy in kept:
        copy.wait()
    for copy in far_copies:
        copy.wait_recv()

    def grads_done(group, carry):
        grad_copy(group).wait()
        return carry

    lax.fori_loop(0, groups, grads_done, 0)
    for copy in started:
        copy.wait_send()


def exchange(pre_keep, pre_send, cotangent, weights, scalars):
    held, tokens, width = pre_keep.shape
    share, columns = cotangent.shape
    slots = weights.shape[0]
    segments = 2 * held
    quarter = held // 2
    half = quarter // 2
    bits = int(math.log2(lax.axis_size("row")))
    members = lax.axis_size("col")
    own = quarter >> (bits - 1)
    staged = 2 * (quarter - own)
    copies = 2 * (members - 1) + 12 + 8 * (bits - 1) + 16 * (quarter // own)
    wide, narrow = jnp.float32, jnp.bfloat16
    pair_shape = (slots // 2, 2 * width, width)
    tiles = columns // width
    out_shape = [jax.ShapeDtypeStruct((segments, tokens, width), narrow)] * 2
    out_shape += [
        jax.ShapeDtypeStruct(pair_shape, narrow),
        jax.ShapeDtypeStruct((share, columns), wide),
    ]
    return pl.pallas_call(
        functools.partial(exchange_kernel, (quarter, own, bits, members)),
        in_specs=[pl.BlockSpec(memory_space=pltpu.SMEM)] * len(scalars)
        + [pl.BlockSpec(memory_space=pl.ANY)] * 4,
        out_specs=[pl.BlockSpec(memory_space=pl.ANY)] * 3
        + [pl.BlockSpec(memory_space=pltpu.VMEM)],
        out_shape=out_shape,
        scratch_shapes=[
            pltpu.VMEM((max(2 * half, GROUP), tokens, width), wide),
            pltpu.VMEM((4 * quarter, tokens, width), narrow),
            pltpu.VMEM((2, half, tokens, width), wide),
            pltpu.VMEM((staged, tokens, width), narrow),
            pltpu.VMEM((2 * staged, tokens, width), narrow),
            pltpu.VMEM((2, own, tokens, width), narrow),
            pltpu.VMEM((2, own, tokens, width), narrow),
            pltpu.VMEM((tokens, columns), narrow),
            pltpu.VMEM((tiles, tokens, width), narrow),
            pltpu.VMEM((AHEAD, GROUP, width, width), narrow),
            pltpu.VMEM((tokens, width), wide),
            pltpu.VMEM((slots, tokens, width), narrow),
            pltpu.VMEM((2, own, tokens, width), wide),
            pltpu.VMEM((tiles, tokens, width), wide),
            pltpu.VMEM((tokens - share, columns), narrow),
            pltpu.VMEM((GROUP, width, width), narrow),
            pltpu.SemaphoreType.DMA((24,)),
            pltpu.SemaphoreType.DMA((AHEAD,)),
            pltpu.SemaphoreType.DMA((slots // GROUP,)),
            pltpu.SemaphoreType.DMA((copies,)),
            pltpu.SemaphoreType.DMA((copies,)),
        ],
        compiler_params=pltpu.CompilerParams(
            collective_id=1, has_side_effects=True, vmem_limit_bytes=EXCHANGE_LIMIT
        ),
        cost_estimate=pl.CostEstimate(
            flops=24 * slots * tokens * width * width,
            bytes_accessed=30 * segments * tokens * width // 2,
            transcendentals=2 * own * tokens * width,
        ),
    )(*scalars, pre_keep, pre_send, cotangent, weights)


def group_order(model, hidden, live, tiles):
    slots = model.shape[0]
    key = jnp.where(live > 0, model, tiles).reshape(-1, GROUP)
    place = jnp.arange(GROUP, dtype=jnp.int32)
    first = (key[:, None, :] < key[:, :, None]) | (
        (key[:, None, :] == key[:, :, None]) & (place[None, :] < place[:, None])
    )
    rank = jnp.sum(first.astype(jnp.int32), axis=2)
    chosen = rank[:, None, :] == place[None, :, None]

    def pick(values):
        return jnp.sum(jnp.where(chosen, values[:, None, :], 0), axis=2)

    spot = jnp.broadcast_to(place[None, :], key.shape)
    ordered = pick(key)
    chain = jnp.concatenate(
        [jnp.zeros_like(ordered[:, :1]), (ordered[:, 1:] == ordered[:, :-1]).astype(jnp.int32)],
        axis=1,
    ).astype(jnp.float32)
    targets = jnp.arange(tiles, dtype=jnp.int32)
    lasts = jnp.max(
        jnp.where(ordered[:, None, :] == targets[None, :, None], spot[:, None, :], -1), axis=2
    )
    ordered_fields = [pick(hidden.reshape(-1, GROUP)), pick(spot), chain, jnp.maximum(lasts, 0)]
    ordered_fields.append((lasts >= 0).astype(jnp.float32))
    return ordered_fields


RELAY_ROWS = 16


def relay_kernel(members, own_ref, all_ref, local_sem, send_sems, recv_sems):
    share = own_ref.shape[0]
    pieces = share // RELAY_ROWS
    me = lax.axis_index("col")
    hops = members - 1

    def place(block, device, piece):
        slot = (block - device + members) % members
        return pl.ds(pl.multiple_of(slot * share + piece * RELAY_ROWS, RELAY_ROWS), RELAY_ROWS)

    mine = pltpu.make_async_copy(own_ref, all_ref.at[pl.ds(0, share)], local_sem)
    mine.start()
    barrier = pltpu.get_barrier_semaphore()
    for step in (1, -1):
        inside = (me + step >= 0) & (me + step < members)

        @pl.when(inside)
        def _():
            pl.semaphore_signal(
                barrier,
                inc=1,
                device_id={"col": me + step},
                device_id_type=pl.DeviceIdType.MESH,
            )

    pl.semaphore_wait(barrier, jnp.where((me > 0) & (me < members - 1), 2, 1))

    def move(side, hop, piece):
        step = 1 if side == 0 else -1
        block = me - step * hop
        target = jnp.clip(me + step, 0, members - 1)
        block = jnp.clip(block, 0, members - 1)
        if hop == 0:
            source = own_ref.at[pl.ds(piece * RELAY_ROWS, RELAY_ROWS)]
        else:
            source = all_ref.at[place(block, me, piece)]
        at = (side * hops + hop) * pieces + piece
        return pltpu.make_async_remote_copy(
            src_ref=source,
            dst_ref=all_ref.at[place(block, target, piece)],
            send_sem=send_sems.at[at],
            recv_sem=recv_sems.at[at],
            device_id={"col": target},
            device_id_type=pl.DeviceIdType.MESH,
        )

    def exists(side, hop):
        step = 1 if side == 0 else -1
        block = me - step * hop
        target = me + step
        return (block >= 0) & (block < members) & (target >= 0) & (target < members)

    def comes(side, hop):
        step = 1 if side == 0 else -1
        block = me - step * (hop + 1)
        return (block >= 0) & (block < members)

    for hop in range(members):
        for piece in range(pieces):
            for side in range(2):
                if hop > 0:

                    @pl.when(comes(side, hop - 1))
                    def _():
                        move(side, hop - 1, piece).wait_recv()

                if hop < hops:

                    @pl.when(exists(side, hop))
                    def _():
                        move(side, hop, piece).start()

    for hop in range(hops):
        for piece in range(pieces):
            for side in range(2):

                @pl.when(exists(side, hop))
                def _():
                    move(side, hop, piece).wait_send()

    mine.wait()


def relay_tokens(values):
    members = lax.axis_size("col")
    share, columns = values.shape
    copies = 2 * (members - 1) * (share // RELAY_ROWS)
    return pl.pallas_call(
        functools.partial(relay_kernel, members),
        in_specs=[pl.BlockSpec(memory_space=pl.ANY)],
        out_specs=pl.BlockSpec(memory_space=pl.ANY),
        out_shape=jax.ShapeDtypeStruct((members * share, columns), values.dtype),
        scratch_shapes=[
            pltpu.SemaphoreType.DMA,
            pltpu.SemaphoreType.DMA((copies,)),
            pltpu.SemaphoreType.DMA((copies,)),
        ],
        compiler_params=pltpu.CompilerParams(collective_id=2, has_side_effects=True),
    )(values)


def shift(values, distance):
    count = lax.axis_size("col")
    return lax.ppermute(values, "col", [(s, (s + distance) % count) for s in range(count)])


def gather_tokens(values):
    count = lax.axis_size("col")
    return jnp.concatenate([values] + [shift(values, -d) for d in range(1, count)], axis=0)


def scatter_tokens(own, send):
    total = own
    for number, piece in enumerate(send):
        total = total + shift(piece, number + 1).astype(jnp.float32)
    return total


def body(activations, grad_out, first_blocks, first_coords, second_blocks, second_coords):
    width = first_blocks.shape[-1]
    members = lax.axis_size("col")
    row_tiles = activations.shape[1] // width
    col_tiles = FF // width // members
    row_base = lax.axis_index("row") * row_tiles
    col_base = lax.axis_index("col") * col_tiles

    def fields(model, hidden):
        is_live = model >= 0
        model_at = jnp.where(is_live, model - row_base, 0)
        hidden_at = jnp.where(is_live, hidden_position(hidden - col_base, col_tiles), 0)
        target = jnp.where(is_live, hidden_at, col_tiles)
        return model_at, hidden_at, target, is_live.astype(jnp.int32)

    model_one, hidden_one, target_one, live_one = fields(
        first_coords[0, 0, :, 0], first_coords[0, 0, :, 1]
    )
    model_two, hidden_two, target_two, live_two = fields(
        second_coords[0, 0, :, 1], second_coords[0, 0, :, 0]
    )
    weights_one = first_blocks[0, 0]
    weights_two = second_blocks[0, 0]

    inputs_all = gather_tokens(activations)
    same = (target_two[1:] == target_two[:-1]).astype(jnp.float32)
    carries = jnp.concatenate([jnp.zeros((1,), jnp.float32), same])
    numbers = jnp.arange(target_two.shape[0], dtype=jnp.int32)
    places = jnp.arange(col_tiles, dtype=jnp.int32)
    lasts = jnp.max(
        jnp.where(target_two[None, :] == places[:, None], numbers[None, :], -1), axis=1
    )
    ends = jnp.maximum(lasts, 0)
    filled = (lasts >= 0).astype(jnp.float32)
    alive_two = live_two.astype(jnp.float32)
    scalars = [model_two, carries, ends, filled, hidden_two, alive_two]
    scalars += group_order(model_two, hidden_two, live_two, grad_out.shape[1] // width)
    source_one, target_one, scalars = lax.optimization_barrier((model_one, target_one, scalars))
    pre_keep, pre_send = to_hidden(inputs_all, weights_one, source_one, target_one, col_tiles)
    _, grad_pre, grads_two, output = exchange(
        pre_keep, pre_send, grad_out, weights_two, scalars
    )
    grad_pre_parts = [grad_pre]
    places_one = (model_one, hidden_one, live_one)
    own_in, send_in = to_model(
        inputs_all,
        grad_pre_parts,
        weights_one,
        places_one,
        members,
        True,
        with_grads=False,
    )
    grad_input = scatter_tokens(own_in, send_in)
    grad_first, grad_second = to_model(
        inputs_all,
        after(grad_pre_parts, own_in, output),
        weights_one,
        places_one,
        members,
        True,
        with_sums=False,
        carried=grads_two,
    )
    grad_second = grad_second.reshape(second_blocks.shape[2:])
    return (output, grad_input, grad_first[None, None], grad_second[None, None])


def solution(mesh):
    return jax.shard_map(
        body,
        mesh=mesh,
        in_specs=(
            P("col", "row"),
            P("col", "row"),
            P("row", "col", None, None, None),
            P("row", "col", None, None),
            P("col", "row", None, None, None),
            P("col", "row", None, None),
        ),
        out_specs=(
            P("col", "row"),
            P("col", "row"),
            P("row", "col", None, None, None),
            P("col", "row", None, None, None),
        ),
        check_vma=False,
    )
```

```python
import functools
import math

import jax
import jax.numpy as jnp
from jax import lax
from jax.experimental import pallas as pl
from jax.experimental.pallas import tpu as pltpu
from jax.sharding import PartitionSpec as P

FF = 65536
CHUNK = 96
VMEM_LIMIT = 58 * 1024 * 1024


def gelu_tanh(values):
    return jax.nn.gelu(values, approximate=True)


def contract(left, right, left_dim, right_dim):
    return lax.dot_general(
        left, right, (((left_dim,), (right_dim,)), ((), ())), preferred_element_type=jnp.float32
    )


def lanes(ref, index, width):
    return ref[:, pl.ds(pl.multiple_of(index * width, width), width)]


OUT_PIECES = 4


def longest_run(slots):
    return next(run for run in (48, 40, 32, 16, 8, 4, 2, 1) if slots % run == 0)


def to_hidden_kernel(source, target, panel, weights, keep, send, totals, blocks, rounded, *sems):
    block_sems, keep_sems, send_sems = sems
    slots, width, _ = weights.shape
    segments = totals.shape[0] - 1
    half = segments // 2
    run = longest_run(slots)
    piece = half // OUT_PIECES

    def load(number):
        here = pl.ds(number * run, run)
        return pltpu.make_async_copy(weights.at[here], blocks.at[here], block_sems.at[number])

    def store(values, number, base, out, out_sems):
        return pltpu.make_async_copy(
            values.at[pl.ds(base + number * piece, piece)],
            out.at[pl.ds(number * piece, piece)],
            out_sems.at[number],
        )

    for number in range(slots // run):
        load(number).start()

    def clear(index, carry):
        totals[index] = jnp.zeros(totals.shape[1:], jnp.float32)
        return carry

    lax.fori_loop(0, segments, clear, 0)

    def add(number, carry):
        load(number).wait()
        for slot in range(run):
            k = number * run + slot
            totals[target[k]] += contract(lanes(panel, source[k], width), blocks[k], 1, 0)
        return carry

    lax.fori_loop(0, slots // run, add, 0)
    for number in range(OUT_PIECES):
        store(totals, number, 0, keep, keep_sems).start()
    for number in range(OUT_PIECES):

        def turn(index, carry):
            at = number * piece + index
            rounded[at] = totals[half + at].astype(jnp.bfloat16)
            return carry

        lax.fori_loop(0, piece, turn, 0)
        store(rounded, number, 0, send, send_sems).start()
    for number in range(OUT_PIECES):
        store(totals, number, 0, keep, keep_sems).wait()
        store(rounded, number, 0, send, send_sems).wait()


def to_hidden(panel, weights, source, target, segments):
    tokens = panel.shape[0]
    slots, width, _ = weights.shape
    half = segments // 2
    return pl.pallas_call(
        to_hidden_kernel,
        grid_spec=pltpu.PrefetchScalarGridSpec(
            num_scalar_prefetch=2,
            grid=(1,),
            in_specs=[
                pl.BlockSpec(panel.shape, lambda s, a, b: (0, 0)),
                pl.BlockSpec(memory_space=pl.ANY),
            ],
            out_specs=[pl.BlockSpec(memory_space=pl.ANY)] * 2,
            scratch_shapes=[
                pltpu.VMEM((segments + 1, tokens, width), jnp.float32),
                pltpu.VMEM((slots, width, width), jnp.bfloat16),
                pltpu.VMEM((half, tokens, width), jnp.bfloat16),
                pltpu.SemaphoreType.DMA((slots // longest_run(slots),)),
                pltpu.SemaphoreType.DMA((OUT_PIECES,)),
                pltpu.SemaphoreType.DMA((OUT_PIECES,)),
            ],
        ),
        out_shape=[
            jax.ShapeDtypeStruct((half, tokens, width), jnp.float32),
            jax.ShapeDtypeStruct((half, tokens, width), jnp.bfloat16),
        ],
        compiler_params=pltpu.CompilerParams(vmem_limit_bytes=VMEM_LIMIT),
        cost_estimate=pl.CostEstimate(
            flops=8 * slots * tokens * width * width,
            bytes_accessed=2 * weights.size + 6 * half * tokens * width,
            transcendentals=0,
        ),
    )(source, target, panel, weights)


FETCHES = 4


def fetch(parts, hidden, sems):
    copies = []
    start = 0
    for part in parts:
        count = part.shape[0] // FETCHES
        for number in range(FETCHES):
            source = part.at[pl.ds(number * count, count)]
            target = hidden.at[pl.ds(start, count)]
            copies.append(pltpu.make_async_copy(source, target, sems.at[len(copies)]))
            copies[-1].start()
            start += count
    for copy in copies:
        copy.wait()


def to_model_kernel(transposed, pieces, with_sums, with_grads, carried, chunk, model_at, hidden_at, live, *refs):
    refs = list(refs)
    panel = refs.pop(0) if with_grads else None
    weights = refs.pop(0) if with_sums else None
    hidden_parts = [refs.pop(0) for _ in range(pieces)]
    carried_in = refs.pop(0) if carried else None
    grads = refs.pop(0) if with_grads else None
    own, send = [refs.pop(0) for _ in range(2)] if with_sums else (None, None)
    carried_out = refs.pop(0) if carried else None
    totals = refs.pop(0) if with_sums else None
    hidden, sems = refs
    step = pl.program_id(0)
    width = hidden.shape[-1]

    @pl.when(step == 0)
    def _():
        if with_sums:
            totals[...] = jnp.zeros(totals.shape, jnp.float32)
        fetch(hidden_parts, hidden, sems)

    if carried:
        carried_out[...] = carried_in[...]

    for slot in range(chunk):
        k = step * chunk + slot
        model = model_at[k]
        values = hidden[hidden_at[k]]
        is_live = live[k] > 0
        if with_sums:
            term = contract(values, weights[slot], 1, 1 if transposed else 0)
            totals[jnp.where(is_live, model, totals.shape[0] - 1)] += term
        if with_grads:
            other = lanes(panel, model, width)
            if transposed:
                grad = contract(other, values, 0, 0)
            else:
                grad = contract(values, other, 0, 0)
            grads[slot] = jnp.where(is_live, grad, 0.0).astype(jnp.bfloat16)

    if with_sums:

        @pl.when(step == pl.num_programs(0) - 1)
        def _():
            share = own.shape[0]
            for segment in range(totals.shape[0] - 1):
                columns = pl.ds(segment * width, width)
                own[:, columns] = totals[segment, pl.ds(0, share), :]
                for number, piece in enumerate(send):
                    rows = pl.ds((number + 1) * share, share)
                    piece[:, columns] = totals[segment, rows, :].astype(jnp.bfloat16)


def to_model(
    panel,
    hidden_parts,
    weights,
    places,
    members,
    transposed,
    with_sums=True,
    with_grads=True,
    carried=None,
):
    tokens, columns = panel.shape
    slots, width, _ = weights.shape
    segments = columns // width
    share = tokens // members
    chunk = next(count for count in (CHUNK, 64, 32, 16, 1) if slots % count == 0)
    hidden_count = sum(part.shape[0] for part in hidden_parts)
    pieces = len(hidden_parts)
    chunk_spec = pl.BlockSpec((chunk, width, width), lambda s, a, b, c: (s, 0, 0))
    share_spec = pl.BlockSpec((share, columns), lambda s, a, b, c: (0, 0))
    operands, in_specs, out_specs, out_shape, scratch = [], [], [], [], []
    if with_grads:
        operands.append(panel)
        in_specs.append(pl.BlockSpec(panel.shape, lambda s, a, b, c: (0, 0)))
        out_specs.append(chunk_spec)
        out_shape.append(jax.ShapeDtypeStruct(weights.shape, jnp.bfloat16))
    if with_sums:
        operands.append(weights)
        in_specs.append(chunk_spec)
        out_specs += [share_spec, [share_spec] * (members - 1)]
        out_shape += [
            jax.ShapeDtypeStruct((share, columns), jnp.float32),
            [jax.ShapeDtypeStruct((share, columns), jnp.bfloat16)] * (members - 1),
        ]
        scratch.append(pltpu.VMEM((segments + 1, tokens, width), jnp.float32))
    scratch += [
        pltpu.VMEM((hidden_count, tokens, width), jnp.bfloat16),
        pltpu.SemaphoreType.DMA((pieces * FETCHES,)),
    ]
    extra, extra_specs = [], []
    if carried is not None:
        extra = [carried]
        carried_spec = pl.BlockSpec(
            (chunk // 2, 2 * width, width), lambda s, a, b, c: (s, 0, 0)
        )
        extra_specs.append(carried_spec)
        out_specs.append(carried_spec)
        out_shape.append(jax.ShapeDtypeStruct(carried.shape, carried.dtype))

    def kernel(*refs):
        flat = list(refs)
        if with_sums:
            start = 3 + len(operands) + pieces + len(extra) + (1 if with_grads else 0) + 1
            if not isinstance(flat[start], (list, tuple)):
                flat[start : start + members - 1] = [flat[start : start + members - 1]]
        to_model_kernel(transposed, pieces, with_sums, with_grads, carried is not None, chunk, *flat)

    return pl.pallas_call(
        kernel,
        grid_spec=pltpu.PrefetchScalarGridSpec(
            num_scalar_prefetch=3,
            grid=(slots // chunk,),
            in_specs=in_specs + [pl.BlockSpec(memory_space=pl.ANY)] * pieces + extra_specs,
            out_specs=out_specs,
            scratch_shapes=scratch,
        ),
        out_shape=out_shape,
        compiler_params=pltpu.CompilerParams(vmem_limit_bytes=VMEM_LIMIT),
        cost_estimate=pl.CostEstimate(
            flops=8 * slots * tokens * width * width * (with_sums + with_grads),
            bytes_accessed=4 * weights.size + 2 * hidden_count * tokens * width,
            transcendentals=0,
        ),
    )(*places, *operands, *hidden_parts, *extra)


def swap(values, bit):
    count = lax.axis_size("row")
    return lax.ppermute(values, "row", [(s, s ^ (1 << bit)) for s in range(count)])


def swap_orders():
    rest = list(range(1, int(math.log2(lax.axis_size("row")))))
    return [rest, rest[::-1]]


def hidden_position(index, segments):
    level = int(math.log2(segments))
    row = lax.axis_index("row")
    masks = []
    for order in swap_orders():
        mask = (row & 1) << (level - 1)
        for number, bit in enumerate(order):
            mask = mask | (((row >> bit) & 1) << (level - 3 - number))
        masks.append(mask)
    is_late = ((index >> (level - 2)) & 1) > 0
    return index ^ jnp.where(is_late, masks[1], masks[0])


def after(values, *earlier):
    return lax.optimization_barrier((values, earlier))[0]


def added(terms, start, count):
    total = None
    for array, base in terms:
        piece = array[base + start : base + start + count].astype(jnp.float32)
        total = piece if total is None else total + piece
    return total


GELU_SCALE = math.sqrt(2.0 / math.pi)


def gelu_and_slope(values):
    square = values * values
    bent = jnp.tanh(GELU_SCALE * (values + 0.044715 * (values * square)))
    half = 0.5 * (1.0 + bent)
    slope = half + (0.5 * GELU_SCALE) * values * (1.0 - bent * bent) * (
        1.0 + (3.0 * 0.044715) * square
    )
    return values * half, slope


GROUP = 32
AHEAD = 2
EXCHANGE_LIMIT = 62 * 1024 * 1024


def exchange_kernel(sizes, *refs):
    quarter, own, bits, members = sizes
    refs = list(refs)
    source_at, carries, ends, filled = refs[0:4]
    hidden_at, alive, sorted_at, block_at, chain, part_ends, part_filled = refs[4:11]
    pre_keep, pre_send, cotangent, weights = refs[11:15]
    hidden, spread_back, grads, output = refs[15:19]
    (parts, hold, back_all, stage_out, stage_in, own_hidden, own_back) = refs[19:26]
    (panel, tiles, blocks, running, sums, slopes, out, landing, chosen) = refs[26:35]
    local_sems, block_sems, grad_sems, send_sems, recv_sems = refs[35:]
    half = quarter // 2
    row = lax.axis_index("row")
    col = lax.axis_index("col")
    orders = [list(range(1, bits)), list(range(1, bits))[::-1]]
    tokens, width = parts.shape[1:]
    acc = [parts.at[pl.ds(n * half, half)] for n in range(2)]
    back = [back_all.at[n] for n in range(2)]
    core_in = [hold.at[pl.ds(n * quarter, quarter)] for n in range(2)]
    back_in = [hold.at[pl.ds((2 + n) * quarter, quarter)] for n in range(2)]
    share = tokens // members
    slots = weights.shape[0]
    groups = slots // GROUP
    strip = 32
    started = []
    counts = [0, 0]

    def local(source, target):
        copy = pltpu.make_async_copy(source, target, local_sems.at[counts[0]])
        counts[0] += 1
        copy.start()
        return copy

    def remote_to(source, target, device):
        copy = pltpu.make_async_remote_copy(
            src_ref=source,
            dst_ref=target,
            send_sem=send_sems.at[counts[1]],
            recv_sem=recv_sems.at[counts[1]],
            device_id=device,
            device_id_type=pl.DeviceIdType.MESH,
        )
        counts[1] += 1
        copy.start()
        started.append(copy)
        return copy

    def remote(source, target, bit):
        return remote_to(source, target, {"row": row ^ (1 << bit)})

    def over(count, step):
        def each(index, carry):
            for start in range(0, tokens, strip):
                step(index, pl.ds(start, strip))
            return carry

        lax.fori_loop(0, count, each, 0)

    def fetch_group(group):
        place = lax.rem(group, AHEAD)
        return pltpu.make_async_copy(
            weights.at[pl.ds(group * GROUP, GROUP)], blocks.at[place], block_sems.at[place]
        )

    loads = [local(pre_keep.at[pl.ds(n * quarter + half, half)], acc[n]) for n in range(2)]
    own_tokens = local(cotangent, panel.at[pl.ds(0, share)])
    for group in range(min(AHEAD, groups)):
        fetch_group(group).start()

    barrier = pltpu.get_barrier_semaphore()
    for bit in range(bits):
        pl.semaphore_signal(
            barrier,
            inc=1,
            device_id={"row": row ^ (1 << bit)},
            device_id_type=pl.DeviceIdType.MESH,
        )
    for distance in range(1, members):
        pl.semaphore_signal(
            barrier,
            inc=1,
            device_id={"col": lax.rem(col + distance, members)},
            device_id_type=pl.DeviceIdType.MESH,
        )
    pl.semaphore_wait(barrier, bits + members - 1)

    low = half // 2
    spans = ((half + low, low), (half, low), (0, half))

    def swap_core(n, span, source, target):
        return remote(source, target[n].at[pl.ds(*span)], 0)

    pre_core = [[], []]
    for span in spans:
        for n in range(2):
            source = pre_send.at[pl.ds(n * quarter + span[0], span[1])]
            pre_core[n].append(swap_core(n, span, source, core_in))
    arrivals = []
    for distance in range(1, members):
        slot = pl.ds((members - distance) * share, share)
        device = {"col": lax.rem(col + distance, members)}
        arrivals.append(remote_to(cotangent, panel.at[slot], device))

    pre_stages = []
    out_places = [0]
    in_places = [0]

    def stage_send(n, bit, count, value, ready):
        base, there = out_places[0], in_places[0]
        out_places[0] += count
        in_places[0] += count
        cut = count // 2
        copies = []
        for number, (start, size) in enumerate(((cut, count - cut), (0, cut))):
            ready[number]()

            def step(index, rows):
                stage_out[base + start + index, rows] = value(start + index, rows).astype(
                    jnp.bfloat16
                )

            over(size, step)
            copies.append(
                remote(
                    stage_out.at[pl.ds(base + start, size)],
                    stage_in.at[pl.ds(there + start, size)],
                    bit,
                )
            )
        pre_stages.append((copies, there))
        return copies, there

    def nothing():
        return None

    def arrived_at(base):
        return lambda i, r: stage_in[base + i, r].astype(jnp.float32)

    def pass_on(ref, n, flight, count, bit):
        copies, base = flight
        lower = count // 2
        copies[0].wait_recv()
        term = arrived_at(base)
        return stage_send(
            n,
            bit,
            lower,
            lambda i, r: ref[n][lower + i, r] + term(lower + i, r),
            (nothing, nothing),
        )

    def fold(ref, n, count, term):
        def step(i, r):
            ref[n][i, r] = ref[n][i, r] + term(i, r)

        over(count, step)

    def fold_rest(ref, n, flight, count):
        copies, base = flight
        copies[1].wait_recv()
        fold(ref, n, count // 2, arrived_at(base))

    def product(group, carry):
        fetch_group(group).wait()
        place = lax.rem(group, AHEAD)
        total = running[...]
        for slot in range(GROUP):
            k = group * GROUP + slot
            term = contract(tiles[source_at[k]], blocks[place, slot], 1, 1)
            total = total * carries[k] + term
            sums[k] = total.astype(jnp.bfloat16)
        running[...] = total

        @pl.when(group + AHEAD < groups)
        def _():
            fetch_group(group + AHEAD).start()

        return carry

    def summed(position, rows):
        return sums[ends[position], rows].astype(jnp.float32) * filled[position]

    def spread(target, n, stages, source, start, size, at, landed, number):
        for later in range(number, len(stages)):
            place = at + start + (own << later)
            copy = remote(source, target.at[pl.ds(place, size)], stages[later])
            landed[later].append((start + (own << later), size, copy))

    def forward(target, n, stages, at, landed, number):
        for start, size, copy in landed[number]:
            copy.wait_recv()
            piece = target.at[pl.ds(at + start, size)]
            spread(target, n, stages, piece, start, size, at, landed, number + 1)

    def cross(source, target, at, start, size):
        far_copies.append(remote(source, target.at[pl.ds(at + start, size)], 0))

    def move_on(target, landed, number):
        for n in range(2):
            at = n * quarter
            forward(target, n, to_hidden_stages[n], at, landed[n], number)
            for start, size, _ in landed[n][number]:
                piece = target.at[pl.ds(at + start, size)]
                cross(piece, target, 2 * quarter + at, start, size)

    far_copies = []
    to_hidden_stages = [order[::-1] for order in orders]
    hidden_landed = [[[] for _ in stages] for stages in to_hidden_stages]
    back_landed = [[[] for _ in stages] for stages in to_hidden_stages]
    cut = own // 2
    own_spans = ((cut, own - cut), (0, cut))

    pre_flight = [None, None]
    for n in range(2):
        loads[n].wait()
        pre_flight[n] = stage_send(
            n,
            orders[n][0],
            half,
            lambda i, r, n=n: acc[n][i, r] + core_in[n][half + i, r].astype(jnp.float32),
            (pre_core[n][0].wait_recv, pre_core[n][1].wait_recv),
        )
        loads[n] = local(pre_keep.at[pl.ds(n * quarter, half)], acc[n])
    for n in range(2):
        loads[n].wait()
        pre_core[n][2].wait_recv()
        fold(acc, n, half, lambda i, r: core_in[n][i, r].astype(jnp.float32))
    running[...] = jnp.zeros(running.shape, jnp.float32)

    count = half
    marks = [0, groups // 3, 2 * groups // 3, groups]
    for number, _ in enumerate(orders[0][1:]):
        flights = [
            pass_on(acc, n, pre_flight[n], count, orders[n][1 + number]) for n in range(2)
        ]
        if number == 0:
            own_tokens.wait()
            for copy in arrivals:
                copy.wait_recv()
            for tile in range(tiles.shape[0]):
                tiles[tile] = panel[:, tile * width : (tile + 1) * width]
            lax.fori_loop(marks[0], marks[1], product, 0)
        for n in range(2):
            fold_rest(acc, n, pre_flight[n], count)
        pre_flight = flights
        count = count // 2
    lax.fori_loop(marks[1], marks[2], product, 0)

    kept = []
    for number, (start, size) in enumerate(own_spans):
        for n in range(2):
            copies, base = pre_flight[n]
            copies[number].wait_recv()

            def act(index, r):
                i = start + index
                value, slope = gelu_and_slope(
                    acc[n][i, r] + stage_in[base + i, r].astype(jnp.float32)
                )
                own_hidden[n, i, r] = value.astype(jnp.bfloat16)
                slopes[n, i, r] = slope

            over(size, act)
            piece = own_hidden.at[n, pl.ds(start, size)]
            at = n * quarter
            spread(
                hidden, n, to_hidden_stages[n], piece, start, size, at, hidden_landed[n], 0
            )
            cross(piece, hidden, 2 * quarter + at, start, size)
            kept.append(local(piece, hidden.at[pl.ds(at + start, size)]))
        if number == 0:
            lax.fori_loop(marks[2], marks[3], product, 0)

    for copies, _ in pre_stages:
        for copy in copies:
            copy.wait_send()
            started[:] = [other for other in started if other is not copy]
    out_places[0] = 0
    back_core = [[], []]
    for first, size in spans:
        for n in range(2):

            def step(i, r):
                value = summed(2 * quarter + n * quarter + first + i, r)
                core_in[n][first + i, r] = value.astype(jnp.bfloat16)

            over(size, step)
            source = core_in[n].at[pl.ds(first, size)]
            back_core[n].append(swap_core(n, (first, size), source, back_in))
    back_flight = [None, None]
    move_on(hidden, hidden_landed, 0)
    for n in range(2):
        back_flight[n] = stage_send(
            n,
            orders[n][0],
            half,
            lambda i, r, n=n: summed(n * quarter + half + i, r)
            + back_in[n][half + i, r].astype(jnp.float32),
            (back_core[n][0].wait_recv, back_core[n][1].wait_recv),
        )
    for n in range(2):
        back_core[n][2].wait_recv()

        def begin(i, r):
            back[n][i, r] = summed(n * quarter + i, r) + back_in[n][i, r].astype(jnp.float32)

        over(half, begin)
    for copies in back_core:
        for copy in copies:
            copy.wait_send()
            started[:] = [other for other in started if other is not copy]

    for number in range(1, len(to_hidden_stages[0])):
        move_on(hidden, hidden_landed, number)
    for copy in kept:
        copy.wait()
    kept.clear()
    for copy in far_copies:
        copy.wait_recv()
    far_copies.clear()
    filled_in = [
        local(hidden.at[pl.ds(n * quarter, quarter)], hold.at[pl.ds(n * quarter, quarter)])
        for n in range(4)
    ]

    out[...] = jnp.zeros(out.shape, jnp.float32)
    pairs = GROUP // 2

    def grad_copy(group):
        here = pl.ds(group * pairs, pairs)
        return pltpu.make_async_copy(sums.at[here], grads.at[here], grad_sems.at[group])

    def forward_product(group, carry):
        fetch_group(group).wait()
        place = lax.rem(group, AHEAD)
        for slot in range(GROUP):
            k = group * GROUP + slot
            grad = contract(hold[hidden_at[k]], tiles[source_at[k]], 0, 0) * alive[k]
            rows = pl.ds(slot % 2 * width, width)
            sums[group * pairs + slot // 2, rows] = grad.astype(jnp.bfloat16)
        grad_copy(group).start()
        for slot in range(GROUP):
            chosen[slot] = blocks[place, slot]
        total = None
        for slot in range(GROUP):
            source = hold[sorted_at[group, slot]]
            term = contract(source, chosen[block_at[group, slot]], 1, 0)
            total = term if slot == 0 else total * chain[group, slot] + term
            parts[slot] = total

        def flush(tile, inner):
            end, factor = part_ends[group, tile], part_filled[group, tile]
            for start in range(0, tokens, strip):
                rows = pl.ds(start, strip)
                out[tile, rows] = out[tile, rows] + parts[end, rows] * factor
            return inner

        lax.fori_loop(0, out.shape[0], flush, 0)

        @pl.when(group + AHEAD < groups)
        def _():
            fetch_group(group + AHEAD).start()

        return carry

    for group in range(min(AHEAD, groups)):
        fetch_group(group).start()
    for copy in filled_in:
        copy.wait()
    steps = [0, groups // 6, groups // 2, 2 * groups // 3, 3 * groups // 4, groups]
    lax.fori_loop(steps[0], steps[1], forward_product, 0)

    count = half
    for number, _ in enumerate(orders[0][1:]):
        flights = [
            pass_on(back, n, back_flight[n], count, orders[n][1 + number]) for n in range(2)
        ]
        if number == 0:
            lax.fori_loop(steps[1], steps[2], forward_product, 0)
        for n in range(2):
            fold_rest(back, n, back_flight[n], count)
        back_flight = flights
        count = count // 2
    lax.fori_loop(steps[2], steps[3], forward_product, 0)

    for number, (start, size) in enumerate(own_spans):
        for n in range(2):
            copies, base = back_flight[n]
            copies[number].wait_recv()

            def slope_times(index, r):
                i = start + index
                value = back[n][i, r] + stage_in[base + i, r].astype(jnp.float32)
                own_back[n, i, r] = (value * slopes[n, i, r]).astype(jnp.bfloat16)

            over(size, slope_times)
            piece = own_back.at[n, pl.ds(start, size)]
            at = n * quarter
            spread(
                spread_back, n, to_hidden_stages[n], piece, start, size, at, back_landed[n], 0
            )
            cross(piece, spread_back, 2 * quarter + at, start, size)
            kept.append(local(piece, spread_back.at[pl.ds(at + start, size)]))
        if number == 0:
            lax.fori_loop(steps[3], steps[4], forward_product, 0)
    lax.fori_loop(steps[4], steps[5], forward_product, 0)

    for tile in range(out.shape[0]):
        panel[:, tile * width : (tile + 1) * width] = out[tile].astype(jnp.bfloat16)
    shares = []
    for distance in range(1, members):
        device = {"col": lax.rem(col + distance, members)}
        source = panel.at[pl.ds(distance * share, share)]
        slot = pl.ds((distance - 1) * share, share)
        shares.append(remote_to(source, landing.at[slot], device))
    for number in range(len(to_hidden_stages[0])):
        move_on(spread_back, back_landed, number)
    for copy in shares:
        copy.wait_recv()
    for tile in range(out.shape[0]):
        columns = slice(tile * width, (tile + 1) * width)
        total = out[tile, 0:share]
        for number in range(members - 1):
            rows = slice(number * share, (number + 1) * share)
            total = total + landing[rows, columns].astype(jnp.float32)
        output[:, columns] = total
    for copy in kept:
        copy.wait()
    for copy in far_copies:
        copy.wait_recv()

    def grads_done(group, carry):
        grad_copy(group).wait()
        return carry

    lax.fori_loop(0, groups, grads_done, 0)
    for copy in started:
        copy.wait_send()


def exchange(pre_keep, pre_send, cotangent, weights, scalars):
    held, tokens, width = pre_keep.shape
    share, columns = cotangent.shape
    slots = weights.shape[0]
    segments = 2 * held
    quarter = held // 2
    half = quarter // 2
    bits = int(math.log2(lax.axis_size("row")))
    members = lax.axis_size("col")
    own = quarter >> (bits - 1)
    staged = 2 * (quarter - own)
    copies = 2 * (members - 1) + 12 + 8 * (bits - 1) + 16 * (quarter // own)
    wide, narrow = jnp.float32, jnp.bfloat16
    pair_shape = (slots // 2, 2 * width, width)
    tiles = columns // width
    out_shape = [jax.ShapeDtypeStruct((segments, tokens, width), narrow)] * 2
    out_shape += [
        jax.ShapeDtypeStruct(pair_shape, narrow),
        jax.ShapeDtypeStruct((share, columns), wide),
    ]
    return pl.pallas_call(
        functools.partial(exchange_kernel, (quarter, own, bits, members)),
        in_specs=[pl.BlockSpec(memory_space=pltpu.SMEM)] * len(scalars)
        + [pl.BlockSpec(memory_space=pl.ANY)] * 4,
        out_specs=[pl.BlockSpec(memory_space=pl.ANY)] * 3
        + [pl.BlockSpec(memory_space=pltpu.VMEM)],
        out_shape=out_shape,
        scratch_shapes=[
            pltpu.VMEM((max(2 * half, GROUP), tokens, width), wide),
            pltpu.VMEM((4 * quarter, tokens, width), narrow),
            pltpu.VMEM((2, half, tokens, width), wide),
            pltpu.VMEM((staged, tokens, width), narrow),
            pltpu.VMEM((2 * staged, tokens, width), narrow),
            pltpu.VMEM((2, own, tokens, width), narrow),
            pltpu.VMEM((2, own, tokens, width), narrow),
            pltpu.VMEM((tokens, columns), narrow),
            pltpu.VMEM((tiles, tokens, width), narrow),
            pltpu.VMEM((AHEAD, GROUP, width, width), narrow),
            pltpu.VMEM((tokens, width), wide),
            pltpu.VMEM((slots, tokens, width), narrow),
            pltpu.VMEM((2, own, tokens, width), wide),
            pltpu.VMEM((tiles, tokens, width), wide),
            pltpu.VMEM((tokens - share, columns), narrow),
            pltpu.VMEM((GROUP, width, width), narrow),
            pltpu.SemaphoreType.DMA((24,)),
            pltpu.SemaphoreType.DMA((AHEAD,)),
            pltpu.SemaphoreType.DMA((slots // GROUP,)),
            pltpu.SemaphoreType.DMA((copies,)),
            pltpu.SemaphoreType.DMA((copies,)),
        ],
        compiler_params=pltpu.CompilerParams(
            collective_id=1, has_side_effects=True, vmem_limit_bytes=EXCHANGE_LIMIT
        ),
        cost_estimate=pl.CostEstimate(
            flops=24 * slots * tokens * width * width,
            bytes_accessed=30 * segments * tokens * width // 2,
            transcendentals=2 * own * tokens * width,
        ),
    )(*scalars, pre_keep, pre_send, cotangent, weights)


def group_order(model, hidden, live, tiles):
    slots = model.shape[0]
    key = jnp.where(live > 0, model, tiles).reshape(-1, GROUP)
    place = jnp.arange(GROUP, dtype=jnp.int32)
    first = (key[:, None, :] < key[:, :, None]) | (
        (key[:, None, :] == key[:, :, None]) & (place[None, :] < place[:, None])
    )
    rank = jnp.sum(first.astype(jnp.int32), axis=2)
    chosen = rank[:, None, :] == place[None, :, None]

    def pick(values):
        return jnp.sum(jnp.where(chosen, values[:, None, :], 0), axis=2)

    spot = jnp.broadcast_to(place[None, :], key.shape)
    ordered = pick(key)
    chain = jnp.concatenate(
        [jnp.zeros_like(ordered[:, :1]), (ordered[:, 1:] == ordered[:, :-1]).astype(jnp.int32)],
        axis=1,
    ).astype(jnp.float32)
    targets = jnp.arange(tiles, dtype=jnp.int32)
    lasts = jnp.max(
        jnp.where(ordered[:, None, :] == targets[None, :, None], spot[:, None, :], -1), axis=2
    )
    ordered_fields = [pick(hidden.reshape(-1, GROUP)), pick(spot), chain, jnp.maximum(lasts, 0)]
    ordered_fields.append((lasts >= 0).astype(jnp.float32))
    return ordered_fields


def shift(values, distance):
    count = lax.axis_size("col")
    return lax.ppermute(values, "col", [(s, (s + distance) % count) for s in range(count)])


def gather_tokens(values):
    count = lax.axis_size("col")
    return jnp.concatenate([values] + [shift(values, -d) for d in range(1, count)], axis=0)


def scatter_tokens(own, send):
    total = own
    for number, piece in enumerate(send):
        total = total + shift(piece, number + 1).astype(jnp.float32)
    return total


def body(activations, grad_out, first_blocks, first_coords, second_blocks, second_coords):
    width = first_blocks.shape[-1]
    members = lax.axis_size("col")
    row_tiles = activations.shape[1] // width
    col_tiles = FF // width // members
    row_base = lax.axis_index("row") * row_tiles
    col_base = lax.axis_index("col") * col_tiles

    def fields(model, hidden):
        is_live = model >= 0
        model_at = jnp.where(is_live, model - row_base, 0)
        hidden_at = jnp.where(is_live, hidden_position(hidden - col_base, col_tiles), 0)
        target = jnp.where(is_live, hidden_at, col_tiles)
        return model_at, hidden_at, target, is_live.astype(jnp.int32)

    model_one, hidden_one, target_one, live_one = fields(
        first_coords[0, 0, :, 0], first_coords[0, 0, :, 1]
    )
    model_two, hidden_two, target_two, live_two = fields(
        second_coords[0, 0, :, 1], second_coords[0, 0, :, 0]
    )
    weights_one = first_blocks[0, 0]
    weights_two = second_blocks[0, 0]

    inputs_all = gather_tokens(activations)
    same = (target_two[1:] == target_two[:-1]).astype(jnp.float32)
    carries = jnp.concatenate([jnp.zeros((1,), jnp.float32), same])
    numbers = jnp.arange(target_two.shape[0], dtype=jnp.int32)
    places = jnp.arange(col_tiles, dtype=jnp.int32)
    lasts = jnp.max(
        jnp.where(target_two[None, :] == places[:, None], numbers[None, :], -1), axis=1
    )
    ends = jnp.maximum(lasts, 0)
    filled = (lasts >= 0).astype(jnp.float32)
    alive_two = live_two.astype(jnp.float32)
    scalars = [model_two, carries, ends, filled, hidden_two, alive_two]
    scalars += group_order(model_two, hidden_two, live_two, grad_out.shape[1] // width)
    source_one, target_one, scalars = lax.optimization_barrier((model_one, target_one, scalars))
    pre_keep, pre_send = to_hidden(inputs_all, weights_one, source_one, target_one, col_tiles)
    _, grad_pre, grads_two, output = exchange(
        pre_keep, pre_send, grad_out, weights_two, scalars
    )
    grad_pre_parts = [grad_pre]
    places_one = (model_one, hidden_one, live_one)
    own_in, send_in = to_model(
        inputs_all,
        grad_pre_parts,
        weights_one,
        places_one,
        members,
        True,
        with_grads=False,
    )
    grad_input = scatter_tokens(own_in, send_in)
    grad_first, grad_second = to_model(
        inputs_all,
        after(grad_pre_parts, own_in, output),
        weights_one,
        places_one,
        members,
        True,
        with_sums=False,
        carried=grads_two,
    )
    grad_second = grad_second.reshape(second_blocks.shape[2:])
    return (output, grad_input, grad_first[None, None], grad_second[None, None])


def solution(mesh):
    return jax.shard_map(
        body,
        mesh=mesh,
        in_specs=(
            P("col", "row"),
            P("col", "row"),
            P("row", "col", None, None, None),
            P("row", "col", None, None),
            P("col", "row", None, None, None),
            P("col", "row", None, None),
        ),
        out_specs=(
            P("col", "row"),
            P("col", "row"),
            P("row", "col", None, None, None),
            P("col", "row", None, None, None),
        ),
        check_vma=False,
    )
```
